256 devices in a mesh: expert: 64 (over x, z, core), hidden: 4 (over y).
Axes of the slice: x: 4, y: 4, z: 8, core: 2. Of those that a mesh axis runs over, the one named last changes fastest.
Arguments:
- pixels: bfloat16 [65536, 1024], P('expert', 'hidden'), may hold values from -6 to 6
- conv_weight: float32 [9, 1024], P(None, 'hidden'), may hold values from -2.5 to 2.5
- norm_gain: float32 [1024], replicated, may hold values from 0.1 to 1.9
- router_weight: bfloat16 [1024, 64], P(None, 'expert'), may hold values from -0.375 to 0.375
- gate_weight: bfloat16 [64, 1024, 4096], P('expert', None, 'hidden'), may hold values from -0.1875 to 0.1875
- up_weight: bfloat16 [64, 1024, 4096], P('expert', None, 'hidden'), may hold values from -0.1875 to 0.1875
- down_weight: bfloat16 [64, 4096, 1024], P('expert', 'hidden'), may hold values from -0.09375 to 0.09375
- expert_ids: int32 [65536, 1], P('expert'), may hold values from 0 to 63; in each aligned block of 1024 rows (0 to 1023, 1024 to 2047, ...) at most 32 rows name the same one
- neighbours: int32 [64, 8], P('expert'), may hold values from -1 to 63, as said below
Outputs:
- block_out: bfloat16 [65536, 1024], P('expert', 'hidden')
The draws below stay inside these ranges and needn't reach their ends.
Inputs may be any that keep to these rules, and one draw needn't show every extreme that they name: `expert_ids`: among the 1024 pixels of one tile (the rows of one device) no expert is named more than 32 times. `neighbours`: A simplified stand-in for the sphere's tile adjacency: the tiles form a grid of 16 rows by 4 columns that closes in the columns; row t lists the tiles to the north, south, west, east, northwest, northeast, southwest and southeast of tile t, and -1 stands for a place beyond the first or last grid row. Which tile stands where is arbitrary.
All inputs are finite; a program needn't handle non-finite values.
Results may differ from the reference program's by a relative error of at most 0.0055.
Values may be sent and summed in bfloat16 or wider, within the bound.
A program may use at most 128 MiB of HBM per device.

```python
import math
import jax
import jax.numpy as jnp
import numpy as np
from jax import lax

D = 1024
FF = 4096
TILE_SIDE = 32
TOK_DEV = 1024
EXPERTS = 64
TILES = 64
PIXELS = 65536
CAP = 32


def draw_neighbours(key, part):
    grid_rows = TILES // 4
    tile_order = jax.random.permutation(key, TILES).astype(jnp.int32)
    position = jnp.arange(TILES, dtype=jnp.int32)
    grid_row = position // 4
    grid_col = position % 4
    offsets = [(-1, 0), (1, 0), (0, -1), (0, 1), (-1, -1), (-1, 1), (1, -1), (1, 1)]
    columns = []
    for row_step, col_step in offsets:
        next_row = grid_row + row_step
        next_col = (grid_col + col_step) % 4
        inside = (next_row >= 0) & (next_row < grid_rows)
        spot = jnp.clip(next_row, 0, grid_rows - 1) * 4 + next_col
        columns.append(jnp.where(inside, tile_order[spot], -1))
    stacked = jnp.stack(columns, axis=1).astype(jnp.int32)
    return jnp.zeros((TILES, 8), jnp.int32).at[tile_order].set(stacked)


def block_levels(rng, shape, cuts, low, largest):
    factor_of = 1.0
    for dim, blocks in cuts:
        draws = jax.random.uniform(jax.random.fold_in(jax.random.fold_in(rng, 6), dim), (blocks,), jnp.float32, low / len(cuts), largest / len(cuts))
        factor_of = factor_of * jnp.repeat(jnp.exp(draws), shape[dim] // blocks).reshape((-1,) + (1,) * (len(shape) - 1 - dim))
    return factor_of


def shared_out(own_key, own, number, rows, number_of, top, limit, skew):
    order = jax.random.permutation(own_key, number_of)
    crowded, usual = shares(number_of, rows * top, limit, skew, True), shares(number_of, rows * top, limit, skew, False)
    places = jnp.arange(number_of)

    def named(lengths, offset_by):
        used = int((lengths > 0).sum())
        fixed = max(1, used // 4)
        moved = fixed + (places - fixed + offset_by * (used - fixed)) % max(1, number_of - fixed)
        return jnp.zeros((number_of,), jnp.int32).at[order[jnp.where(places < fixed, places, moved)]].set(jnp.asarray(lengths, jnp.int32))

    lengths = jnp.where(number % 4 == 0, named(crowded, number // 4), named(usual, number - number // 4 - 1))
    mixed = jax.random.permutation(jax.random.fold_in(own, 3), number_of)
    source_of, taker = mixed[0:number_of // 2 * 2:2], mixed[1:number_of // 2 * 2:2]
    margin = jnp.minimum(lengths[source_of] - 1, limit - lengths[taker]) // 2
    margin = jnp.where((source_of == order[0]) | (taker == order[0]) | (lengths[taker] == 0), 0, jnp.maximum(margin, 0))
    moved = jax.random.randint(jax.random.fold_in(own, 4), (number_of // 2,), 0, 1 << 20) % (margin + 1)
    lengths = lengths.at[source_of].add(-moved).at[taker].add(moved)
    members = jnp.searchsorted(jnp.cumsum(lengths), jnp.arange(rows * top), side="right").astype(jnp.int32)
    listing = members.reshape(top, rows).T
    listing = listing[jax.random.permutation(jax.random.fold_in(own, 1), rows)]
    offset_by = jax.random.randint(jax.random.fold_in(own, 2), (rows, 1), 0, top)
    return jnp.take_along_axis(listing, (jnp.arange(top)[None, :] + offset_by) % top, axis=1)


def shares(number_of, total, most, skew, full):
    loads = [(1 << 20) // math.isqrt(grade ** skew) + 1 for grade in range(1, number_of + 1)]
    largest = most if full else min(most, max(-(-total // number_of), total * loads[0] // sum(loads)))
    least = 1 if total - largest >= number_of - 1 else 0
    given, surplus = [largest] + [least] * (number_of - 1), total - largest - least * (number_of - 1)
    while surplus > 0:
        candidates = [i for i in range(1, number_of) if given[i] < largest] or [i for i in range(1, number_of) if given[i] < most]
        mass, budget = sum([loads[i] for i in candidates]), surplus
        for i in candidates:
            addition = min(most - given[i], max(1, budget * loads[i] // mass), surplus)
            given[i] = given[i] + addition
            surplus = surplus - addition
    return np.array(given)


def gaussian(own_key, dims, width, most, cuts=(), kind=jnp.bfloat16):
    values = jax.random.normal(own_key, dims, jnp.float32) * width
    if len(cuts) > 0:
        values = block_levels(own_key, dims, cuts, -0.22, 0.18) * values
    return jnp.clip(values, min=-most, max=most).astype(kind)


def setup_inputs(seed: int = 0) -> dict:
    key_of = jax.random.split(jax.random.key(seed), 10)
    pixels = gaussian(key_of[0], (PIXELS, D), 1.0, 6.0, ((0, 64), (1, 4)))
    conv_weight = gaussian(key_of[1], (9, D), 0.35, 2.5, ((1, 4),), jnp.float32)
    norm_gain = jnp.clip(1.0 + 0.18 * jax.random.normal(key_of[2], (D,), jnp.float32), 0.1, 1.9)
    router_weight = gaussian(key_of[3], (D, EXPERTS), (D // 4) ** -0.5, 0.375, ((1, 64),))
    gate_weight = gaussian(key_of[4], (EXPERTS, D, FF), D ** -0.5, 0.1875, ((0, 64), (2, 4)))
    up_weight = gaussian(key_of[5], (EXPERTS, D, FF), D ** -0.5, 0.1875, ((0, 64), (2, 4)))
    down_weight = gaussian(key_of[6], (EXPERTS, FF, D), FF ** -0.5, 0.09375, ((0, 64), (1, 4)))
    expert_ids_keys = jax.random.split(jax.random.fold_in(key_of[7], 1), PIXELS // TOK_DEV)
    expert_ids_turns = jax.random.permutation(jax.random.fold_in(key_of[7], 3), PIXELS // TOK_DEV)
    expert_ids = jax.vmap(lambda own, number: shared_out(jax.random.fold_in(key_of[7], 2), own, number, TOK_DEV, EXPERTS, 1, CAP, 2))(expert_ids_keys, expert_ids_turns).reshape((PIXELS, 1))
    neighbours = draw_neighbours(jax.random.fold_in(key_of[9], 71), 0)
    return dict(pixels=pixels, conv_weight=conv_weight, norm_gain=norm_gain, router_weight=router_weight, gate_weight=gate_weight, up_weight=up_weight, down_weight=down_weight, expert_ids=expert_ids, neighbours=neighbours)


epsilon = 1e-05

def reference(pixels, conv_weight, norm_gain, router_weight, gate_weight, up_weight, down_weight, expert_ids, neighbours):
    tile_side = TILE_SIDE
    tiles = pixels.astype(jnp.float32).reshape(TILES, tile_side, tile_side, D)
    present = (neighbours >= 0).astype(jnp.float32)
    source_tile = jnp.maximum(neighbours, 0).astype(jnp.int32)

    def fetch_rim(edge, direction):
        picked = edge[source_tile[:, direction]]
        return picked * present[:, direction].reshape((TILES,) + (1,) * (edge.ndim - 1))
    north = fetch_rim(tiles[:, tile_side - 1], 0)
    south = fetch_rim(tiles[:, 0], 1)
    west = fetch_rim(tiles[:, :, tile_side - 1], 2)
    east = fetch_rim(tiles[:, :, 0], 3)
    corner_nw = fetch_rim(tiles[:, tile_side - 1, tile_side - 1], 4)
    corner_ne = fetch_rim(tiles[:, tile_side - 1, 0], 5)
    corner_sw = fetch_rim(tiles[:, 0, tile_side - 1], 6)
    corner_se = fetch_rim(tiles[:, 0, 0], 7)
    upper_rim = jnp.concatenate([corner_nw[:, None], north, corner_ne[:, None]], axis=1)
    lower_rim = jnp.concatenate([corner_sw[:, None], south, corner_se[:, None]], axis=1)
    middle = jnp.concatenate([west[:, :, None], tiles, east[:, :, None]], axis=2)
    padded = jnp.concatenate([upper_rim[:, None], middle, lower_rim[:, None]], axis=1)
    mixed = tiles
    for row_off in range(3):
        for col_off in range(3):
            mixed = mixed + conv_weight[3 * row_off + col_off] * padded[:, row_off:row_off + tile_side, col_off:col_off + tile_side]
    conv_out = mixed.astype(jnp.bfloat16).reshape(PIXELS, D)
    wide_feats = conv_out.astype(jnp.float32)
    mean_sq = lax.optimization_barrier(jnp.mean(wide_feats * wide_feats, axis=1, keepdims=True))
    normed = (wide_feats * lax.rsqrt(mean_sq + epsilon) * norm_gain).astype(jnp.bfloat16)
    expert_of = expert_ids[:, 0].astype(jnp.int32)
    onehot = (expert_of[:, None] == jnp.arange(EXPERTS, dtype=jnp.int32)[None]).astype(jnp.int32)
    onehot = onehot.reshape(TILES, TOK_DEV, EXPERTS)
    ranks = jnp.cumsum(onehot, axis=1) - onehot
    slot_index = lax.optimization_barrier(jnp.sum(ranks * onehot, axis=2)).reshape(PIXELS).astype(jnp.int32)
    tile_of = (jnp.arange(PIXELS, dtype=jnp.int32) // TOK_DEV).astype(jnp.int32)
    position = (tile_of * CAP + slot_index).astype(jnp.int32)
    logits = jnp.dot(normed, router_weight, preferred_element_type=jnp.float32)
    weight = jax.nn.sigmoid(jnp.take_along_axis(logits, expert_of[:, None], axis=1))
    buffer_rows = TILES * CAP

    def per_expert(accum, expert_index):
        routed = expert_of == expert_index
        target = jnp.where(routed, position, buffer_rows).astype(jnp.int32)
        buffer = jnp.zeros((buffer_rows, D), jnp.bfloat16).at[target].set(normed, mode='drop')
        gate_buffer = jnp.zeros((buffer_rows, 1), jnp.float32).at[target].set(weight, mode='drop')
        gate_act = jnp.dot(buffer, gate_weight[expert_index], preferred_element_type=jnp.float32)
        up_act = jnp.dot(buffer, up_weight[expert_index], preferred_element_type=jnp.float32)
        hidden = (jax.nn.silu(gate_act) * up_act * gate_buffer).astype(jnp.bfloat16)
        result = jnp.dot(hidden, down_weight[expert_index], preferred_element_type=jnp.float32).astype(jnp.bfloat16)
        fetched = result[jnp.minimum(target, buffer_rows - 1)].astype(jnp.float32)
        accum = accum + jnp.where(routed[:, None], fetched, jnp.zeros_like(fetched))
        return (accum, None)
    expert_sum, unused = lax.scan(per_expert, jnp.zeros((PIXELS, D), jnp.float32), jnp.arange(EXPERTS, dtype=jnp.int32))
    return (conv_out.astype(jnp.float32) + expert_sum).astype(jnp.bfloat16)
```

```python
import jax
import jax.numpy as jnp
from jax import lax
from jax.experimental import pallas as pl
from jax.experimental.pallas import tpu as pltpu
from jax.sharding import PartitionSpec as P

MESH = pl.DeviceIdType.MESH
F32 = jnp.float32
BF16 = jnp.bfloat16

SIDE = 32
TOKENS = SIDE * SIDE
EXPERTS = 64
CAP = 32
OWN = 256
PARTS = 4
UNITS = 1024
WIDTH = OWN * PARTS
GROUPS = 8
BLOCKS = EXPERTS // GROUPS
HALF = BLOCKS // 2
ROWS = BLOCKS * CAP
LEFT = 8
EPSILON = 1e-05


def kernel(
    pixels,
    conv_weight,
    norm_gain,
    router,
    ids,
    table,
    gate_hbm,
    up_hbm,
    down_hbm,
    out,
    padded,
    rim_out,
    rim_in,
    pick_out,
    pick_in,
    conv,
    place_row,
    place_col,
    router_wide,
    gate_w,
    up_w,
    down_w,
    outgoing,
    rows,
    normed,
    hidden,
    partial,
    relay_dn,
    relay_up,
    sums_dn,
    sums_up,
    final,
    returned,
    total,
    weight_sem,
    send_sem,
    rim_sem,
    disp_sem,
    gat_dn,
    gat_up,
    fwd_dn,
    fwd_up,
    rel_dn,
    rel_up,
    sum_dn,
    sum_up,
    ret_sem,
):
    e = lax.axis_index("expert")
    y = lax.axis_index("hidden")
    x, z, c = lax.div(e, 16), lax.rem(lax.div(e, 2), 8), lax.rem(e, 2)
    up, dn, op = lax.rem(y + 1, 4), lax.rem(y + 3, 4), lax.rem(y + 2, 4)

    def ahead(k):
        dx, dc, dz = lax.div(k, 16), lax.rem(lax.div(k, 8), 2), lax.rem(k, 8)
        return (lax.rem(x + dx, 4) * 8 + lax.rem(z + dz, 8)) * 2 + lax.rem(c + dc, 2)

    def behind(k):
        dx, dc, dz = lax.div(k, 16), lax.rem(lax.div(k, 8), 2), lax.rem(k, 8)
        return (lax.rem(x + 4 - dx, 4) * 8 + lax.rem(z + 8 - dz, 8)) * 2 + lax.rem(c + dc, 2)

    def remote(src, dst, sent, got, target):
        return pltpu.make_async_remote_copy(
            src_ref=src,
            dst_ref=dst,
            send_sem=sent,
            recv_sem=got,
            device_id=target,
            device_id_type=MESH,
        )

    def received(dst, sem):
        remote(dst, dst, send_sem.at[0], sem, (e, up)).wait_recv()

    def sent(src, sem):
        remote(src, src, sem, rim_sem.at[0], (e, up)).wait_send()

    barrier = pltpu.get_barrier_semaphore()

    def greet(k, carry):
        pl.semaphore_signal(barrier, inc=1, device_id=(ahead(k), y), device_id_type=MESH)
        return carry

    lax.fori_loop(1, EXPERTS, greet, 0)
    pl.semaphore_signal(barrier, inc=1, device_id=(e, up), device_id_type=MESH)
    pl.semaphore_signal(barrier, inc=1, device_id=(e, dn), device_id_type=MESH)

    loads = [
        pltpu.make_async_copy(gate_hbm.at[0], gate_w, weight_sem.at[0]),
        pltpu.make_async_copy(up_hbm.at[0], up_w, weight_sem.at[1]),
        pltpu.make_async_copy(down_hbm.at[0], down_w, weight_sem.at[2]),
    ]
    for load in loads:
        load.start()

    def widen(i, carry):
        at = pl.multiple_of(i * SIDE, SIDE)
        padded[i + 1, LEFT : LEFT + SIDE, :] = pixels[pl.ds(at, SIDE), :].astype(F32)
        return carry

    lax.fori_loop(0, SIDE, widen, 0)
    rim_out[...] = jnp.zeros_like(rim_out)
    near, far = LEFT, LEFT + SIDE - 1
    for half in range(2):
        lanes = slice(128 * half, 128 * half + 128)
        at = slice(SIDE * half, SIDE * half + SIDE)
        rim_out[at, 0, :] = padded[1, near : far + 1, lanes]
        rim_out[at, 1, :] = padded[SIDE, near : far + 1, lanes]
        rim_out[at, 2, :] = padded[1 : SIDE + 1, near, lanes]
        rim_out[at, 3, :] = padded[1 : SIDE + 1, far, lanes]
    rim_out[:, 4, 0:8] = jnp.broadcast_to(table[...].astype(F32), (EXPERTS, 8))

    pl.semaphore_wait(barrier, EXPERTS - 1 + 2)

    def send_rim(k, carry):
        target = ahead(k)
        remote(
            rim_out.at[target], rim_in.at[e], send_sem.at[0], rim_sem.at[0], (target, y)
        ).start()
        return carry

    lax.fori_loop(1, EXPERTS, send_rim, 0)
    rim_in[e] = rim_out[e]

    onehot = (
        ids[...] == lax.broadcasted_iota(jnp.int32, (EXPERTS, TOKENS), 0)
    ).astype(F32)
    onehot_bf = onehot.astype(BF16)

    def places(b, carry):
        at = pl.multiple_of(b * 256, 256)
        earlier = lax.broadcasted_iota(jnp.int32, (TOKENS, 256), 0) < (
            lax.broadcasted_iota(jnp.int32, (TOKENS, 256), 1) + at
        )
        counts = jnp.dot(
            onehot_bf, earlier.astype(F32).astype(BF16), preferred_element_type=F32
        )
        own = ids[0:1, pl.ds(at, 256)]
        chosen = own == lax.broadcasted_iota(jnp.int32, (EXPERTS, 256), 0)
        slot = jnp.sum(jnp.where(chosen, counts, 0.0), axis=0, keepdims=True)
        dx = (lax.shift_right_logical(own, 4) - x + 4) & 3
        dz = ((lax.shift_right_logical(own, 1) & 7) - z + 8) & 7
        dc = ((own & 1) + c) & 1
        place = (dx * 16 + dc * 8 + dz).astype(F32) * CAP + slot
        place_row[0:1, pl.ds(at, 256)] = place
        place_col[pl.ds(at, 256), :] = jnp.broadcast_to(place, (128, 256)).T
        return carry

    lax.fori_loop(0, TOKENS // 256, places, 0)

    def widen_router(b, carry):
        at = pl.multiple_of(b * 256, 256)
        column = router[0:1, pl.ds(at, 256)].astype(F32)
        router_wide[pl.ds(at, 256), :] = jnp.broadcast_to(column, (128, 256)).T.astype(BF16)
        return carry

    lax.fori_loop(0, WIDTH // 256, widen_router, 0)

    received(rim_in.at[pl.ds(0, EXPERTS - 1)], rim_sem.at[0])
    tables = rim_in[:, 4, :]
    tile = lax.broadcasted_iota(jnp.int32, (EXPERTS, EXPERTS), 1).astype(F32)
    edges = [rim_in[:, edge, :].astype(BF16) for edge in range(4)]
    for direction, edge in enumerate((1, 0, 3, 2, 1, 1, 0, 0)):
        chosen = (tables[:, direction : direction + 1] == tile).astype(F32).astype(BF16)
        pick_out[:, direction, :] = jnp.dot(chosen, edges[edge], preferred_element_type=F32)

    def send_pick(k, carry):
        target = ahead(k)
        remote(
            pick_out.at[target], pick_in.at[e], send_sem.at[1], rim_sem.at[1], (target, y)
        ).start()
        return carry

    lax.fori_loop(1, EXPERTS, send_pick, 0)
    pick_in[e] = pick_out[e]
    received(pick_in.at[pl.ds(0, EXPERTS - 1)], rim_sem.at[1])

    for half in range(2):
        lanes = slice(128 * half, 128 * half + 128)
        at = slice(SIDE * half, SIDE * half + SIDE)
        first, last = SIDE * half, SIDE * half + SIDE - 1
        padded[0, near : far + 1, lanes] = pick_in[at, 0, :]
        padded[SIDE + 1, near : far + 1, lanes] = pick_in[at, 1, :]
        padded[1 : SIDE + 1, near - 1, lanes] = pick_in[at, 2, :]
        padded[1 : SIDE + 1, far + 1, lanes] = pick_in[at, 3, :]
        padded[0, near - 1 : near, lanes] = pick_in[last, 4:5, :]
        padded[0, far + 1 : far + 2, lanes] = pick_in[first, 5:6, :]
        padded[SIDE + 1, near - 1 : near, lanes] = pick_in[last, 6:7, :]
        padded[SIDE + 1, far + 1 : far + 2, lanes] = pick_in[first, 7:8, :]

    def convolve(i, carry):
        mixed = padded[i + 1, near : far + 1, :]
        for a in range(3):
            for b in range(3):
                tap = conv_weight[3 * a + b : 3 * a + b + 1, :]
                mixed = mixed + tap * padded[i + a, near - 1 + b : far + b, :]
        conv[pl.ds(pl.multiple_of(i * SIDE, SIDE), SIDE), :] = mixed.astype(BF16)
        return carry

    lax.fori_loop(0, SIDE, convolve, 0)
    total[...] = jnp.zeros_like(total)

    def dispatch(g):
        first = lax.broadcasted_iota(jnp.int32, (ROWS, TOKENS), 0) + g * ROWS
        chosen = (place_row[...] == first.astype(F32)).astype(F32).astype(BF16)
        block = jnp.dot(chosen, conv[...], preferred_element_type=F32).astype(BF16)
        outgoing[pl.ds(g * BLOCKS, BLOCKS)] = block.reshape(BLOCKS, CAP, OWN)

        @pl.when(g == 0)
        def _():
            pltpu.make_async_copy(outgoing.at[0], rows.at[y, 0], disp_sem.at[0]).start()

        def send(k, carry):
            remote(
                outgoing.at[k], rows.at[y, k], send_sem.at[2], disp_sem.at[g], (ahead(k), y)
            ).start()
            return carry

        lax.fori_loop(jnp.where(g == 0, 1, g * BLOCKS), (g + 1) * BLOCKS, send, 0)

    def gather(g):
        span = pl.ds(g * BLOCKS, BLOCKS)
        mine = rows.at[y, span]
        received(mine, disp_sem.at[g])
        remote(mine, mine, send_sem.at[3], gat_dn.at[g], (e, up)).start()
        remote(mine, mine, send_sem.at[4], gat_up.at[g], (e, dn)).start()

    def forward(g):
        received(rows.at[dn, pl.ds(g * BLOCKS, BLOCKS)], gat_dn.at[g])
        low = rows.at[dn, pl.ds(g * BLOCKS, HALF)]
        remote(low, low, send_sem.at[5], fwd_dn.at[g], (e, up)).start()
        received(rows.at[up, pl.ds(g * BLOCKS, BLOCKS)], gat_up.at[g])
        high = rows.at[up, pl.ds(g * BLOCKS + HALF, HALF)]
        remote(high, high, send_sem.at[6], fwd_up.at[g], (e, dn)).start()

    def expert(g):
        received(rows.at[op, pl.ds(g * BLOCKS, HALF)], fwd_dn.at[g])
        received(rows.at[op, pl.ds(g * BLOCKS + HALF, HALF)], fwd_up.at[g])
        span = pl.ds(g * BLOCKS, BLOCKS)
        squares = jnp.zeros((ROWS, 1), F32)
        for part in range(PARTS):
            wide = rows[part, span].reshape(ROWS, OWN).astype(F32)
            squares = squares + jnp.sum(wide * wide, axis=1, keepdims=True)
        scale = lax.rsqrt(squares * (1.0 / WIDTH) + EPSILON)
        for part in range(PARTS):
            wide = rows[part, span].reshape(ROWS, OWN).astype(F32)
            normed[:, part * OWN : (part + 1) * OWN] = (
                wide * scale * norm_gain[part : part + 1, :]
            ).astype(BF16)
        score = jnp.dot(normed[...], router_wide[...], preferred_element_type=F32)
        weight = 1.0 / (1.0 + jnp.exp(-score))
        weight = jnp.concatenate([weight, weight], axis=1)

        def units(n, carry):
            at = pl.ds(pl.multiple_of(n * 256, 256), 256)
            gate = jnp.dot(normed[...], gate_w[:, at], preferred_element_type=F32)
            lift = jnp.dot(normed[...], up_w[:, at], preferred_element_type=F32)
            hidden[:, at] = (gate / (1.0 + jnp.exp(-gate)) * lift * weight).astype(BF16)
            return carry

        lax.fori_loop(0, UNITS // 256, units, 0)

        def channels(part, carry):
            at = pl.ds(pl.multiple_of(part * OWN, OWN), OWN)
            result = jnp.dot(hidden[...], down_w[:, at], preferred_element_type=F32)
            partial[part, span] = result.astype(BF16).reshape(BLOCKS, CAP, OWN)
            return carry

        lax.fori_loop(0, PARTS, channels, 0)

        low, high = pl.ds(g * BLOCKS, HALF), pl.ds(g * BLOCKS + HALF, HALF)
        slot = pl.ds(g * HALF, HALF)
        remote(
            partial.at[op, low], relay_dn.at[slot], send_sem.at[7], rel_dn.at[g], (e, up)
        ).start()
        remote(
            partial.at[op, high], relay_up.at[slot], send_sem.at[8], rel_up.at[g], (e, dn)
        ).start()
        remote(
            partial.at[up, high], sums_dn.at[high], send_sem.at[9], sum_dn.at[g], (e, up)
        ).start()
        remote(
            partial.at[dn, low], sums_up.at[low], send_sem.at[10], sum_up.at[g], (e, dn)
        ).start()

    def relay(g):
        low, high = pl.ds(g * BLOCKS, HALF), pl.ds(g * BLOCKS + HALF, HALF)
        slot = pl.ds(g * HALF, HALF)
        received(relay_dn.at[slot], rel_dn.at[g])
        partial[up, low] = (partial[up, low].astype(F32) + relay_dn[slot].astype(F32)).astype(BF16)
        remote(
            partial.at[up, low], sums_dn.at[low], send_sem.at[9], sum_dn.at[g], (e, up)
        ).start()
        received(relay_up.at[slot], rel_up.at[g])
        partial[dn, high] = (
            partial[dn, high].astype(F32) + relay_up[slot].astype(F32)
        ).astype(BF16)
        remote(
            partial.at[dn, high], sums_up.at[high], send_sem.at[10], sum_up.at[g], (e, dn)
        ).start()

    def give_back(g):
        span = pl.ds(g * BLOCKS, BLOCKS)
        received(sums_dn.at[span], sum_dn.at[g])
        received(sums_up.at[span], sum_up.at[g])
        final[span] = (
            partial[y, span].astype(F32) + sums_dn[span].astype(F32) + sums_up[span].astype(F32)
        ).astype(BF16)

        @pl.when(g == 0)
        def _():
            pltpu.make_async_copy(final.at[0], returned.at[0], ret_sem.at[0]).start()

        def send(k, carry):
            remote(
                final.at[k], returned.at[k], send_sem.at[11], ret_sem.at[g], (behind(k), y)
            ).start()
            return carry

        lax.fori_loop(jnp.where(g == 0, 1, g * BLOCKS), (g + 1) * BLOCKS, send, 0)

    def combine(g):
        span = pl.ds(g * BLOCKS, BLOCKS)
        received(returned.at[span], ret_sem.at[g])
        block = returned[span].reshape(ROWS, OWN)
        number = (lax.broadcasted_iota(jnp.int32, (256, 128), 1) + g * ROWS).astype(F32)

        def add(b, carry):
            at = pl.ds(pl.multiple_of(b * 256, 256), 256)
            place = place_col[at, :]
            chosen = jnp.concatenate(
                [(place == number).astype(F32), (place == number + 128.0).astype(F32)], axis=1
            ).astype(BF16)
            total[at, :] += jnp.dot(chosen, block, preferred_element_type=F32)
            return carry

        lax.fori_loop(0, TOKENS // 256, add, 0)

    dispatch(0)
    dispatch(1)
    for load in loads:
        load.wait()

    def step(s, carry):
        pl.when(s < GROUPS)(lambda: gather(s))
        pl.when(s + 2 < GROUPS)(lambda: dispatch(s + 2))
        pl.when((s >= 1) & (s < GROUPS + 1))(lambda: forward(s - 1))
        pl.when((s >= 2) & (s < GROUPS + 2))(lambda: expert(s - 2))
        pl.when((s >= 3) & (s < GROUPS + 3))(lambda: relay(s - 3))
        pl.when((s >= 4) & (s < GROUPS + 4))(lambda: give_back(s - 4))
        pl.when(s >= 5)(lambda: combine(s - 5))
        return carry

    lax.fori_loop(0, GROUPS + 5, step, 0)
    out[...] = (conv[...].astype(F32) + total[...]).astype(BF16)

    most, half = pl.ds(0, EXPERTS - 1), pl.ds(0, EXPERTS // 2)
    sent(rim_out.at[most], send_sem.at[0])
    sent(pick_out.at[most], send_sem.at[1])
    sent(outgoing.at[most], send_sem.at[2])
    sent(outgoing, send_sem.at[3])
    sent(outgoing, send_sem.at[4])
    sent(outgoing.at[half], send_sem.at[5])
    sent(outgoing.at[half], send_sem.at[6])
    sent(outgoing.at[half], send_sem.at[7])
    sent(outgoing.at[half], send_sem.at[8])
    sent(outgoing, send_sem.at[9])
    sent(outgoing, send_sem.at[10])
    sent(final.at[most], send_sem.at[11])


def shards(
    pixels,
    conv_weight,
    norm_gain,
    router_weight,
    gate_weight,
    up_weight,
    down_weight,
    expert_ids,
    neighbours,
):
    vmem = pl.BlockSpec(memory_space=pltpu.VMEM)
    hbm = pl.BlockSpec(memory_space=pltpu.HBM)
    blocks = (EXPERTS, CAP, OWN)
    per_group = pltpu.SemaphoreType.DMA((GROUPS,))
    return pl.pallas_call(
        kernel,
        out_shape=jax.ShapeDtypeStruct((TOKENS, OWN), BF16),
        in_specs=[vmem] * 6 + [hbm] * 3,
        out_specs=vmem,
        scratch_shapes=[
            pltpu.VMEM((SIDE + 2, SIDE + 2 * LEFT, OWN), F32),
            pltpu.VMEM((EXPERTS, 8, 128), F32),
            pltpu.VMEM((EXPERTS, 8, 128), F32),
            pltpu.VMEM((EXPERTS, 8, 128), F32),
            pltpu.VMEM((EXPERTS, 8, 128), F32),
            pltpu.VMEM((TOKENS, OWN), BF16),
            pltpu.VMEM((1, TOKENS), F32),
            pltpu.VMEM((TOKENS, 128), F32),
            pltpu.VMEM((WIDTH, 128), BF16),
            pltpu.VMEM((WIDTH, UNITS), BF16),
            pltpu.VMEM((WIDTH, UNITS), BF16),
            pltpu.VMEM((UNITS, WIDTH), BF16),
            pltpu.VMEM(blocks, BF16),
            pltpu.VMEM((PARTS,) + blocks, BF16),
            pltpu.VMEM((ROWS, WIDTH), BF16),
            pltpu.VMEM((ROWS, UNITS), BF16),
            pltpu.VMEM((PARTS,) + blocks, BF16),
            pltpu.VMEM((EXPERTS // 2, CAP, OWN), BF16),
            pltpu.VMEM((EXPERTS // 2, CAP, OWN), BF16),
            pltpu.VMEM(blocks, BF16),
            pltpu.VMEM(blocks, BF16),
            pltpu.VMEM(blocks, BF16),
            pltpu.VMEM(blocks, BF16),
            pltpu.VMEM((TOKENS, OWN), F32),
            pltpu.SemaphoreType.DMA((3,)),
            pltpu.SemaphoreType.DMA((12,)),
            pltpu.SemaphoreType.DMA((2,)),
        ]
        + [per_group] * 10,
        compiler_params=pltpu.CompilerParams(
            collective_id=0, has_side_effects=True, vmem_limit_bytes=48 * 1024 * 1024
        ),
    )(
        pixels,
        conv_weight,
        norm_gain.reshape(PARTS, OWN),
        router_weight.reshape(1, WIDTH),
        expert_ids.reshape(1, TOKENS),
        neighbours,
        gate_weight,
        up_weight,
        down_weight,
    )


def solution(mesh):
    in_specs = (
        P("expert", "hidden"),
        P(None, "hidden"),
        P(),
        P(None, "expert"),
        P("expert", None, "hidden"),
        P("expert", None, "hidden"),
        P("expert", "hidden", None),
        P("expert", None),
        P("expert", None),
    )
    out_specs = P("expert", "hidden")
    return jax.shard_map(shards, mesh=mesh, in_specs=in_specs, out_specs=out_specs, check_vma=False)
```

```python
import jax
import jax.numpy as jnp
from jax import lax
from jax.experimental import pallas as pl
from jax.experimental.pallas import tpu as pltpu
from jax.sharding import PartitionSpec as P

MESH = pl.DeviceIdType.MESH
F32 = jnp.float32
BF16 = jnp.bfloat16

SIDE = 32
TOKENS = SIDE * SIDE
EXPERTS = 64
CAP = 32
OWN = 256
PARTS = 4
UNITS = 1024
WIDTH = OWN * PARTS
GROUPS = 8
BLOCKS = EXPERTS // GROUPS
HALF = BLOCKS // 2
ROWS = BLOCKS * CAP
CHIPS = EXPERTS // 2
EDGE = 4 * SIDE
INNER = TOKENS - 2 * SIDE
OWN_BLOCK = 24
LEFT = 8
EPSILON = 1e-05


def kernel(
    pixels,
    conv_weight,
    norm_gain,
    router,
    ids,
    table,
    gate_hbm,
    up_hbm,
    down_hbm,
    out,
    pixels_in,
    taps,
    gain_in,
    router_in,
    ids_in,
    table_in,
    padded,
    rim_wide,
    rim_out,
    rim_in,
    held,
    pick_wide,
    pick_out,
    pick_in,
    conv,
    parts_row,
    place_row,
    place_col,
    router_wide,
    gate_w,
    up_w,
    down_w,
    outgoing,
    rows,
    normed,
    hidden,
    partial,
    relay_dn,
    relay_up,
    sums_dn,
    sums_up,
    final,
    returned,
    total,
    load_sem,
    send_sem,
    rim_sem,
    src_sem,
    disp_sem,
    gat_dn,
    gat_up,
    fwd_dn,
    fwd_up,
    rel_dn,
    rel_up,
    sum_dn,
    sum_up,
    ret_sem,
):
    e = lax.axis_index("expert")
    y = lax.axis_index("hidden")
    x, z, c = lax.div(e, 16), lax.rem(lax.div(e, 2), 8), lax.rem(e, 2)
    chip = lax.div(e, 2)
    up, dn, op = lax.rem(y + 1, 4), lax.rem(y + 3, 4), lax.rem(y + 2, 4)

    def is_near(g):
        return (g == 3) | (g == 5) | (g == 7)

    def offsets(k):
        g, i = lax.div(k, BLOCKS), lax.rem(k, BLOCKS)
        turn = jnp.where(
            is_near(g), lax.div(g + 5, 2) - 4, jnp.where(g < 3, g, jnp.where(g == 4, 3, 4))
        )
        third = lax.rem(i + turn, 3)
        dz = jnp.where(is_near(g), jnp.where(third == 2, 7, third), 2 + lax.rem(i + turn, 5))
        return lax.div(i, 2), lax.rem(i, 2), dz

    def ahead(k):
        dx, dc, dz = offsets(k)
        return (lax.rem(x + dx, 4) * 8 + lax.rem(z + dz, 8)) * 2 + lax.rem(c + dc, 2)

    def behind(k):
        dx, dc, dz = offsets(k)
        return (lax.rem(x + 4 - dx, 4) * 8 + lax.rem(z + 8 - dz, 8)) * 2 + lax.rem(c + dc, 2)

    def chip_ahead(k):
        return lax.rem(x + lax.div(k, 8), 4) * 8 + lax.rem(z + lax.rem(k, 8), 8)

    def remote(src, dst, sent, got, target):
        return pltpu.make_async_remote_copy(
            src_ref=src,
            dst_ref=dst,
            send_sem=sent,
            recv_sem=got,
            device_id=target,
            device_id_type=MESH,
        )

    def received(dst, sem):
        remote(dst, dst, send_sem.at[0], sem, (e, up)).wait_recv()

    def sent(src, sem):
        remote(src, src, sem, rim_sem.at[0], (e, up)).wait_send()

    loads = [
        pltpu.make_async_copy(source, target, load_sem.at[i])
        for i, (source, target) in enumerate(
            (
                (pixels, pixels_in),
                (table, table_in),
                (ids, ids_in),
                (router, router_in),
                (conv_weight, taps),
                (norm_gain, gain_in),
                (gate_hbm.at[0], gate_w),
                (up_hbm.at[0], up_w),
                (down_hbm.at[0], down_w),
            )
        )
    ]
    for load in loads:
        load.start()

    barrier = pltpu.get_barrier_semaphore()

    def greet(k, carry):
        target = lax.rem(e + k, EXPERTS)
        pl.semaphore_signal(barrier, inc=1, device_id=(target, y), device_id_type=MESH)
        return carry

    lax.fori_loop(1, EXPERTS, greet, 0)
    pl.semaphore_signal(barrier, inc=1, device_id=(e, up), device_id_type=MESH)
    pl.semaphore_signal(barrier, inc=1, device_id=(e, dn), device_id_type=MESH)

    padded[...] = jnp.zeros_like(padded)
    rim_wide[...] = jnp.zeros_like(rim_wide)
    conv[:, 0:SIDE] = jnp.zeros((PARTS, SIDE, OWN), BF16)
    conv[:, TOKENS - SIDE : TOKENS] = jnp.zeros((PARTS, SIDE, OWN), BF16)
    for load in loads[:6]:
        load.wait()

    def widen(i, carry):
        at = pl.multiple_of(i * SIDE, SIDE)
        padded[i + 1, LEFT : LEFT + SIDE, :] = pixels_in[pl.ds(at, SIDE), :].astype(F32)
        return carry

    lax.fori_loop(0, SIDE, widen, 0)
    near, far = LEFT, LEFT + SIDE - 1
    for half in range(2):
        lanes = slice(128 * half, 128 * half + 128)
        rim_wide[:, half, :] = padded[1, near : far + 1, lanes]
        rim_wide[:, 2 + half, :] = padded[SIDE, near : far + 1, lanes]
        rim_wide[:, 4 + half, :] = padded[1 : SIDE + 1, near, lanes]
        rim_wide[:, 6 + half, :] = padded[1 : SIDE + 1, far, lanes]
    rim_wide[:, 8, 0:8] = jnp.broadcast_to(table_in[...].astype(F32), (CHIPS, 8))
    rim_out[...] = rim_wide[...].astype(BF16)
    rim_in[c, chip] = rim_out[chip]

    def convolve(i, carry):
        mixed = padded[i + 1, near : far + 1, :]
        for a in range(3):
            for b in range(3):
                tap = taps[3 * a + b : 3 * a + b + 1, :]
                mixed = mixed + tap * padded[i + a, near - 1 + b : far + b, :]
        rounded = mixed.astype(BF16)
        conv[y, pl.ds(pl.multiple_of(i * SIDE, SIDE), SIDE), :] = rounded
        total[i] = rounded.astype(F32)
        return carry

    lax.fori_loop(0, SIDE, convolve, 0)

    pl.semaphore_wait(barrier, EXPERTS - 1 + 2)

    def send_rim(k, carry):
        target = chip_ahead(k)
        remote(
            rim_out.at[target],
            rim_in.at[c, chip],
            send_sem.at[0],
            rim_sem.at[0],
            (target * 2 + c, y),
        ).start()
        return carry

    lax.fori_loop(1, CHIPS, send_rim, 0)

    first_half, second_half = pl.ds(SIDE, INNER // 2), pl.ds(SIDE + INNER // 2, INNER // 2)
    remote(
        conv.at[y, first_half], conv.at[y, first_half], send_sem.at[12], src_sem.at[0], (e, up)
    ).start()
    remote(
        conv.at[y, second_half], conv.at[y, second_half], send_sem.at[12], src_sem.at[1], (e, dn)
    ).start()
    remote(
        conv.at[y, second_half], conv.at[y, second_half], send_sem.at[12], src_sem.at[2], (e, up)
    ).start()
    remote(
        conv.at[y, first_half], conv.at[y, first_half], send_sem.at[12], src_sem.at[3], (e, dn)
    ).start()

    onehot = (
        ids_in[...] == lax.broadcasted_iota(jnp.int32, (EXPERTS, TOKENS), 0)
    ).astype(F32)
    onehot_bf = onehot.astype(BF16)
    parts_row[...] = jnp.zeros_like(parts_row)

    def places(b, carry):
        at = pl.multiple_of(b * 256, 256)
        earlier = lax.broadcasted_iota(jnp.int32, (TOKENS, 256), 0) < (
            lax.broadcasted_iota(jnp.int32, (TOKENS, 256), 1) + at
        )
        counts = jnp.dot(
            onehot_bf, earlier.astype(F32).astype(BF16), preferred_element_type=F32
        )
        own = ids_in[0:1, pl.ds(at, 256)]
        chosen = own == lax.broadcasted_iota(jnp.int32, (EXPERTS, 256), 0)
        slot = jnp.sum(jnp.where(chosen, counts, 0.0), axis=0, keepdims=True)
        dx = (lax.shift_right_logical(own, 4) - x + 4) & 3
        dz = ((lax.shift_right_logical(own, 1) & 7) - z + 8) & 7
        dc = ((own & 1) + c) & 1
        i = dx * 2 + dc
        third = jnp.where(dz == 7, 2, dz) + 9 - i
        third = jnp.where(third >= 6, third - 6, third)
        third = jnp.where(third >= 3, third - 3, third)
        fifth = dz + 8 - i
        fifth = jnp.where(fifth >= 10, fifth - 10, jnp.where(fifth >= 5, fifth - 5, fifth))
        is_close = (dz <= 1) | (dz == 7)
        group = jnp.where(
            is_close, 3 + 2 * third, jnp.where(fifth < 3, fifth, 2 * fifth - 2)
        )
        block = (group * BLOCKS + i).astype(F32)
        place = block * CAP + slot
        number = lax.broadcasted_iota(jnp.int32, (1, 256), 1) + at
        row, column = lax.shift_right_logical(number, 5), number & 31
        inner = (row >= 1) & (row <= SIDE - 2) & (column >= 1) & (column <= SIDE - 2)
        place_row[0:1, pl.ds(at, 256)] = jnp.where(inner, place, -1.0)
        parts_row[0:1, pl.ds(at, 256)] = block
        parts_row[1:2, pl.ds(at, 256)] = slot
        place_col[pl.ds(at, 256), :] = jnp.broadcast_to(place, (128, 256)).T
        return carry

    lax.fori_loop(0, TOKENS // 256, places, 0)

    number = lax.broadcasted_iota(jnp.int32, (1, EDGE), 1)
    along = number & 31
    edge = lax.shift_right_logical(number, 5)
    pixel = jnp.where(
        edge == 0,
        along,
        jnp.where(
            edge == 1,
            along + (TOKENS - SIDE),
            jnp.where(edge == 2, along * SIDE, along * SIDE + SIDE - 1),
        ),
    )
    picks = (lax.broadcasted_iota(jnp.int32, (TOKENS, EDGE), 0) == pixel).astype(F32).astype(BF16)
    border = jnp.dot(parts_row[...].astype(BF16), picks, preferred_element_type=F32)
    counted = (edge <= 1) | ((along >= 1) & (along <= SIDE - 2))
    place_row[0:1, TOKENS : TOKENS + EDGE] = jnp.where(
        counted, border[0:1] * CAP + border[1:2], -1.0
    )

    def widen_router(b, carry):
        at = pl.multiple_of(b * 256, 256)
        column = router_in[0:1, pl.ds(at, 256)].astype(F32)
        router_wide[pl.ds(at, 256), :] = jnp.broadcast_to(column, (128, 256)).T.astype(BF16)
        return carry

    received(rim_in.at[c, pl.ds(0, CHIPS - 1)], rim_sem.at[0])
    other = e + 1 - 2 * c
    remote(rim_in.at[c], rim_in.at[c], send_sem.at[13], rim_sem.at[2], (other, y)).start()
    held[c] = rim_in[c].astype(F32)
    received(rim_in.at[1 - c], rim_sem.at[2])
    held[1 - c] = rim_in[1 - c].astype(F32)
    tables = held[c, :, 8, :]
    tile = lax.broadcasted_iota(jnp.int32, (CHIPS, EXPERTS), 1)
    tile = ((tile & 31) * 2 + lax.shift_right_logical(tile, 5)).astype(F32)
    edges = [
        jnp.concatenate(
            [
                jnp.concatenate([held[core, :, 2 * side + half, :] for half in range(2)], axis=1)
                for core in range(2)
            ],
            axis=0,
        ).astype(BF16)
        for side in range(4)
    ]
    for direction, side in enumerate((1, 0, 3, 2, 1, 1, 0, 0)):
        chosen = (tables[:, direction : direction + 1] == tile).astype(F32).astype(BF16)
        found = jnp.dot(chosen, edges[side], preferred_element_type=F32)
        pick_wide[:, 2 * direction, :] = found[:, 0:128]
        pick_wide[:, 2 * direction + 1, :] = found[:, 128:256]
    pick_out[...] = pick_wide[...].astype(BF16)

    def send_pick(k, carry):
        target = chip_ahead(k)
        remote(
            pick_out.at[target],
            pick_in.at[chip],
            send_sem.at[1],
            rim_sem.at[1],
            (target * 2 + c, y),
        ).start()
        return carry

    lax.fori_loop(1, CHIPS, send_pick, 0)
    pick_in[chip] = pick_out[chip]

    lax.fori_loop(0, WIDTH // 256, widen_router, 0)
    received(conv.at[dn, first_half], src_sem.at[0])
    remote(
        conv.at[dn, first_half], conv.at[dn, first_half], send_sem.at[14], src_sem.at[4], (e, up)
    ).start()
    received(conv.at[up, second_half], src_sem.at[1])
    remote(
        conv.at[up, second_half], conv.at[up, second_half], send_sem.at[14], src_sem.at[5], (e, dn)
    ).start()

    received(pick_in.at[pl.ds(0, CHIPS - 1)], rim_sem.at[1])
    pick_wide[...] = pick_in[...].astype(F32)
    for half in range(2):
        lanes = slice(128 * half, 128 * half + 128)
        padded[0, near : far + 1, lanes] = pick_wide[:, half, :]
        padded[SIDE + 1, near : far + 1, lanes] = pick_wide[:, 2 + half, :]
        padded[1 : SIDE + 1, near - 1, lanes] = pick_wide[:, 4 + half, :]
        padded[1 : SIDE + 1, far + 1, lanes] = pick_wide[:, 6 + half, :]
        last = SIDE - 1
        padded[0, near - 1 : near, lanes] = pick_wide[last, 8 + half : 9 + half, :]
        padded[0, far + 1 : far + 2, lanes] = pick_wide[0, 10 + half : 11 + half, :]
        padded[SIDE + 1, near - 1 : near, lanes] = pick_wide[last, 12 + half : 13 + half, :]
        padded[SIDE + 1, far + 1 : far + 2, lanes] = pick_wide[0, 14 + half : 15 + half, :]

    def mix(center, window):
        mixed = center
        for a in range(3):
            for b in range(3):
                mixed = mixed + taps[3 * a + b : 3 * a + b + 1, :] * window(a, b)
        return mixed.astype(BF16)

    left = mix(
        padded[1 : SIDE + 1, near, :], lambda a, b: padded[a : a + SIDE, near - 1 + b, :]
    )
    right = mix(padded[1 : SIDE + 1, far, :], lambda a, b: padded[a : a + SIDE, far - 1 + b, :])
    top = mix(padded[1, near : far + 1, :], lambda a, b: padded[a, near - 1 + b : far + b, :])
    bottom = mix(
        padded[SIDE, near : far + 1, :],
        lambda a, b: padded[SIDE - 1 + a, near - 1 + b : far + b, :],
    )
    for i, strip in enumerate((top, bottom, left, right)):
        conv[y, TOKENS + i * SIDE : TOKENS + (i + 1) * SIDE, :] = strip
    total[:, 0, :] = left.astype(F32)
    total[:, SIDE - 1, :] = right.astype(F32)
    total[0] = top.astype(F32)
    total[SIDE - 1] = bottom.astype(F32)

    def blocks_of(g):
        first = lax.broadcasted_iota(jnp.int32, (ROWS, TOKENS + EDGE), 0) + g * ROWS
        return (place_row[...] == first.astype(F32)).astype(F32).astype(BF16)

    def dispatch_far(g):
        block = jnp.dot(blocks_of(g), conv[y], preferred_element_type=F32).astype(BF16)
        outgoing[y, pl.ds(g * BLOCKS, BLOCKS)] = block.reshape(BLOCKS, CAP, OWN)

        def send(k, carry):
            remote(
                outgoing.at[y, k], rows.at[y, k], send_sem.at[2], disp_sem.at[g], (ahead(k), y)
            ).start()
            return carry

        lax.fori_loop(g * BLOCKS, (g + 1) * BLOCKS, send, 0)

    def dispatch_near(g):
        chosen = blocks_of(g)
        for part in range(PARTS):
            block = jnp.dot(chosen, conv[part], preferred_element_type=F32).astype(BF16)
            outgoing[part, pl.ds(g * BLOCKS, BLOCKS)] = block.reshape(BLOCKS, CAP, OWN)

        @pl.when(g == 3)
        def _():
            pltpu.make_async_copy(
                outgoing.at[:, OWN_BLOCK], rows.at[:, OWN_BLOCK], disp_sem.at[3]
            ).start()

        def send(k, carry):
            remote(
                outgoing.at[:, k], rows.at[:, k], send_sem.at[15], disp_sem.at[g], (ahead(k), y)
            ).start()
            return carry

        lax.fori_loop(g * BLOCKS + jnp.where(g == 3, 1, 0), (g + 1) * BLOCKS, send, 0)

    pack = pl.ds(TOKENS, EDGE)
    pack_low, pack_high = pl.ds(TOKENS, EDGE // 2), pl.ds(TOKENS + EDGE // 2, EDGE // 2)

    def forward_pack():
        received(conv.at[dn, pack], src_sem.at[6])
        remote(
            conv.at[dn, pack_low], conv.at[dn, pack_low], send_sem.at[17], src_sem.at[8], (e, up)
        ).start()
        received(conv.at[up, pack], src_sem.at[7])
        remote(
            conv.at[up, pack_high], conv.at[up, pack_high], send_sem.at[17], src_sem.at[9], (e, dn)
        ).start()

    def conv_complete():
        received(conv.at[dn, second_half], src_sem.at[2])
        received(conv.at[up, first_half], src_sem.at[3])
        received(conv.at[op, first_half], src_sem.at[4])
        received(conv.at[op, second_half], src_sem.at[5])
        received(conv.at[op, pack_low], src_sem.at[8])
        received(conv.at[op, pack_high], src_sem.at[9])

    def gather(g):
        span = pl.ds(g * BLOCKS, BLOCKS)
        mine = rows.at[y, span]
        received(mine, disp_sem.at[g])
        remote(mine, mine, send_sem.at[3], gat_dn.at[g], (e, up)).start()
        remote(mine, mine, send_sem.at[4], gat_up.at[g], (e, dn)).start()

    def forward(g):
        received(rows.at[dn, pl.ds(g * BLOCKS, BLOCKS)], gat_dn.at[g])
        low = rows.at[dn, pl.ds(g * BLOCKS, HALF)]
        remote(low, low, send_sem.at[5], fwd_dn.at[g], (e, up)).start()
        received(rows.at[up, pl.ds(g * BLOCKS, BLOCKS)], gat_up.at[g])
        high = rows.at[up, pl.ds(g * BLOCKS + HALF, HALF)]
        remote(high, high, send_sem.at[6], fwd_up.at[g], (e, dn)).start()

    def arrived(g):
        received(rows.at[op, pl.ds(g * BLOCKS, HALF)], fwd_dn.at[g])
        received(rows.at[op, pl.ds(g * BLOCKS + HALF, HALF)], fwd_up.at[g])

    def expert(g):
        span = pl.ds(g * BLOCKS, BLOCKS)
        pl.when(is_near(g))(lambda: received(rows.at[:, span], disp_sem.at[g]))
        pl.when(jnp.logical_not(is_near(g)))(lambda: arrived(g))
        squares = jnp.zeros((ROWS, 1), F32)
        for part in range(PARTS):
            wide = rows[part, span].reshape(ROWS, OWN).astype(F32)
            squares = squares + jnp.sum(wide * wide, axis=1, keepdims=True)
        scale = lax.rsqrt(squares * (1.0 / WIDTH) + EPSILON)
        for part in range(PARTS):
            wide = rows[part, span].reshape(ROWS, OWN).astype(F32)
            normed[:, part * OWN : (part + 1) * OWN] = (
                wide * scale * gain_in[0:1, part * OWN : (part + 1) * OWN]
            ).astype(BF16)
        score = jnp.dot(normed[...], router_wide[...], preferred_element_type=F32)
        weight = 1.0 / (1.0 + jnp.exp(-score))
        weight = jnp.concatenate([weight, weight], axis=1)

        def units(n, carry):
            at = pl.ds(pl.multiple_of(n * 256, 256), 256)
            gate = jnp.dot(normed[...], gate_w[:, at], preferred_element_type=F32)
            lift = jnp.dot(normed[...], up_w[:, at], preferred_element_type=F32)
            hidden[:, at] = (gate / (1.0 + jnp.exp(-gate)) * lift * weight).astype(BF16)
            return carry

        lax.fori_loop(0, UNITS // 256, units, 0)

        def channels(part, carry):
            at = pl.ds(pl.multiple_of(part * OWN, OWN), OWN)
            result = jnp.dot(hidden[...], down_w[:, at], preferred_element_type=F32)
            partial[part, span] = result.astype(BF16).reshape(BLOCKS, CAP, OWN)
            return carry

        lax.fori_loop(0, PARTS, channels, 0)

        low, high = pl.ds(g * BLOCKS, HALF), pl.ds(g * BLOCKS + HALF, HALF)
        slot = pl.ds(g * HALF, HALF)
        remote(
            partial.at[op, low], relay_dn.at[slot], send_sem.at[7], rel_dn.at[g], (e, up)
        ).start()
        remote(
            partial.at[op, high], relay_up.at[slot], send_sem.at[8], rel_up.at[g], (e, dn)
        ).start()
        remote(
            partial.at[up, high], sums_dn.at[high], send_sem.at[9], sum_dn.at[g], (e, up)
        ).start()
        remote(
            partial.at[dn, low], sums_up.at[low], send_sem.at[10], sum_up.at[g], (e, dn)
        ).start()

    def relay(g):
        low, high = pl.ds(g * BLOCKS, HALF), pl.ds(g * BLOCKS + HALF, HALF)
        slot = pl.ds(g * HALF, HALF)
        received(relay_dn.at[slot], rel_dn.at[g])
        partial[up, low] = (partial[up, low].astype(F32) + relay_dn[slot].astype(F32)).astype(BF16)
        remote(
            partial.at[up, low], sums_dn.at[low], send_sem.at[9], sum_dn.at[g], (e, up)
        ).start()
        received(relay_up.at[slot], rel_up.at[g])
        partial[dn, high] = (
            partial[dn, high].astype(F32) + relay_up[slot].astype(F32)
        ).astype(BF16)
        remote(
            partial.at[dn, high], sums_up.at[high], send_sem.at[10], sum_up.at[g], (e, dn)
        ).start()

    def give_back(g):
        span = pl.ds(g * BLOCKS, BLOCKS)
        received(sums_dn.at[span], sum_dn.at[g])
        received(sums_up.at[span], sum_up.at[g])
        final[span] = (
            partial[y, span].astype(F32) + sums_dn[span].astype(F32) + sums_up[span].astype(F32)
        ).astype(BF16)

        @pl.when(g == 3)
        def _():
            pltpu.make_async_copy(
                final.at[OWN_BLOCK], returned.at[OWN_BLOCK], ret_sem.at[3]
            ).start()

        def send(k, carry):
            remote(
                final.at[k], returned.at[k], send_sem.at[11], ret_sem.at[g], (behind(k), y)
            ).start()
            return carry

        lax.fori_loop(g * BLOCKS + jnp.where(g == 3, 1, 0), (g + 1) * BLOCKS, send, 0)

    def combine(g):
        span = pl.ds(g * BLOCKS, BLOCKS)
        received(returned.at[span], ret_sem.at[g])
        block = returned[span].reshape(ROWS, OWN)
        number = (lax.broadcasted_iota(jnp.int32, (256, 128), 1) + g * ROWS).astype(F32)

        def add(b, carry):
            at = pl.ds(pl.multiple_of(b * 256, 256), 256)
            place = place_col[at, :]
            chosen = jnp.concatenate(
                [(place == number).astype(F32), (place == number + 128.0).astype(F32)], axis=1
            ).astype(BF16)
            tile_rows = pl.ds(b * 8, 8)
            added = jnp.dot(chosen, block, preferred_element_type=F32)
            total[tile_rows] += added.reshape(8, SIDE, OWN)
            return carry

        lax.fori_loop(0, TOKENS // 256, add, 0)

    dispatch_far(0)
    remote(conv.at[y, pack], conv.at[y, pack], send_sem.at[16], src_sem.at[6], (e, up)).start()
    remote(conv.at[y, pack], conv.at[y, pack], send_sem.at[16], src_sem.at[7], (e, dn)).start()
    dispatch_far(1)
    for load in loads[6:]:
        load.wait()

    def step(s, carry):
        pl.when((s < GROUPS) & jnp.logical_not(is_near(s)))(lambda: gather(s))
        pl.when(s == 0)(forward_pack)
        pl.when(s == 1)(conv_complete)
        pl.when((s + 2 < GROUPS) & is_near(s + 2))(lambda: dispatch_near(s + 2))
        pl.when((s + 2 < GROUPS) & jnp.logical_not(is_near(s + 2)))(lambda: dispatch_far(s + 2))
        pl.when((s >= 1) & (s < GROUPS + 1) & jnp.logical_not(is_near(s - 1)))(
            lambda: forward(s - 1)
        )
        pl.when((s >= 2) & (s < GROUPS + 2))(lambda: expert(s - 2))
        pl.when((s >= 3) & (s < GROUPS + 3))(lambda: relay(s - 3))
        pl.when((s >= 4) & (s < GROUPS + 4))(lambda: give_back(s - 4))
        pl.when(s >= 5)(lambda: combine(s - 5))
        return carry

    lax.fori_loop(0, GROUPS + 5, step, 0)
    out[...] = total[...].reshape(TOKENS, OWN).astype(BF16)

    def span_of(count):
        return outgoing.at[0, pl.ds(0, count)]

    sent(rim_out.at[pl.ds(0, CHIPS - 1)], send_sem.at[0])
    sent(pick_out.at[pl.ds(0, CHIPS - 1)], send_sem.at[1])
    sent(rim_in.at[0], send_sem.at[13])
    sent(span_of(40), send_sem.at[2])
    sent(span_of(40), send_sem.at[3])
    sent(span_of(40), send_sem.at[4])
    sent(span_of(20), send_sem.at[5])
    sent(span_of(20), send_sem.at[6])
    sent(span_of(32), send_sem.at[7])
    sent(span_of(32), send_sem.at[8])
    sent(span_of(64), send_sem.at[9])
    sent(span_of(64), send_sem.at[10])
    sent(span_of(63), send_sem.at[11])
    sent(conv.at[pl.ds(0, 2), pl.ds(0, INNER)], send_sem.at[12])
    sent(conv.at[0, pl.ds(0, INNER)], send_sem.at[14])
    sent(outgoing.at[:, pl.ds(0, 23)], send_sem.at[15])
    sent(conv.at[0, pl.ds(0, 2 * EDGE)], send_sem.at[16])
    sent(conv.at[0, pl.ds(0, EDGE)], send_sem.at[17])


def shards(
    pixels,
    conv_weight,
    norm_gain,
    router_weight,
    gate_weight,
    up_weight,
    down_weight,
    expert_ids,
    neighbours,
):
    vmem = pl.BlockSpec(memory_space=pltpu.VMEM)
    hbm = pl.BlockSpec(memory_space=pltpu.HBM)
    blocks = (EXPERTS, CAP, OWN)
    per_group = pltpu.SemaphoreType.DMA((GROUPS,))
    return pl.pallas_call(
        kernel,
        out_shape=jax.ShapeDtypeStruct((TOKENS, OWN), BF16),
        in_specs=[hbm] * 9,
        out_specs=vmem,
        scratch_shapes=[
            pltpu.VMEM((TOKENS, OWN), BF16),
            pltpu.VMEM((9, OWN), F32),
            pltpu.VMEM((1, WIDTH), F32),
            pltpu.VMEM((1, WIDTH), BF16),
            pltpu.VMEM((1, TOKENS), jnp.int32),
            pltpu.VMEM((1, 8), jnp.int32),
            pltpu.VMEM((SIDE + 2, SIDE + 2 * LEFT, OWN), F32),
            pltpu.VMEM((CHIPS, 16, 128), F32),
            pltpu.VMEM((CHIPS, 16, 128), BF16),
            pltpu.VMEM((2, CHIPS, 16, 128), BF16),
            pltpu.VMEM((2, CHIPS, 16, 128), F32),
            pltpu.VMEM((CHIPS, 16, 128), F32),
            pltpu.VMEM((CHIPS, 16, 128), BF16),
            pltpu.VMEM((CHIPS, 16, 128), BF16),
            pltpu.VMEM((PARTS, TOKENS + EDGE, OWN), BF16),
            pltpu.VMEM((8, TOKENS), F32),
            pltpu.VMEM((1, TOKENS + EDGE), F32),
            pltpu.VMEM((TOKENS, 128), F32),
            pltpu.VMEM((WIDTH, 128), BF16),
            pltpu.VMEM((WIDTH, UNITS), BF16),
            pltpu.VMEM((WIDTH, UNITS), BF16),
            pltpu.VMEM((UNITS, WIDTH), BF16),
            pltpu.VMEM((PARTS,) + blocks, BF16),
            pltpu.VMEM((PARTS,) + blocks, BF16),
            pltpu.VMEM((ROWS, WIDTH), BF16),
            pltpu.VMEM((ROWS, UNITS), BF16),
            pltpu.VMEM((PARTS,) + blocks, BF16),
            pltpu.VMEM((EXPERTS // 2, CAP, OWN), BF16),
            pltpu.VMEM((EXPERTS // 2, CAP, OWN), BF16),
            pltpu.VMEM(blocks, BF16),
            pltpu.VMEM(blocks, BF16),
            pltpu.VMEM(blocks, BF16),
            pltpu.VMEM(blocks, BF16),
            pltpu.VMEM((SIDE, SIDE, OWN), F32),
            pltpu.SemaphoreType.DMA((9,)),
            pltpu.SemaphoreType.DMA((18,)),
            pltpu.SemaphoreType.DMA((3,)),
            pltpu.SemaphoreType.DMA((10,)),
        ]
        + [per_group] * 10,
        compiler_params=pltpu.CompilerParams(
            collective_id=0, has_side_effects=True, vmem_limit_bytes=63 * 1024 * 1024
        ),
    )(
        pixels,
        conv_weight,
        norm_gain.reshape(1, WIDTH),
        router_weight.reshape(1, WIDTH),
        expert_ids.reshape(1, TOKENS),
        neighbours,
        gate_weight,
        up_weight,
        down_weight,
    )


def solution(mesh):
    in_specs = (
        P("expert", "hidden"),
        P(None, "hidden"),
        P(),
        P(None, "expert"),
        P("expert", None, "hidden"),
        P("expert", None, "hidden"),
        P("expert", "hidden", None),
        P("expert", None),
        P("expert", None),
    )
    out_specs = P("expert", "hidden")
    return jax.shard_map(shards, mesh=mesh, in_specs=in_specs, out_specs=out_specs, check_vma=False)
```

```python
import jax
import jax.numpy as jnp
from jax import lax
from jax.experimental import pallas as pl
from jax.experimental.pallas import tpu as pltpu
from jax.sharding import PartitionSpec as P

MESH = pl.DeviceIdType.MESH
F32 = jnp.float32
BF16 = jnp.bfloat16

SIDE = 32
TOKENS = SIDE * SIDE
EXPERTS = 64
CAP = 32
OWN = 256
PARTS = 4
UNITS = 1024
WIDTH = OWN * PARTS
GROUPS = 8
BLOCKS = EXPERTS // GROUPS
HALF = BLOCKS // 2
ROWS = BLOCKS * CAP
CHIPS = EXPERTS // 2
EDGE = 4 * SIDE
INNER = TOKENS - 2 * SIDE
OWN_BLOCK = 24
LEFT = 8
EPSILON = 1e-05


def kernel(
    pixels,
    conv_weight,
    norm_gain,
    router,
    ids,
    table,
    gate_hbm,
    up_hbm,
    down_hbm,
    out,
    pixels_in,
    taps,
    gain_in,
    router_in,
    ids_in,
    table_in,
    padded,
    rim_wide,
    rim_out,
    rim_in,
    held,
    pick_wide,
    pick_out,
    pick_in,
    conv,
    parts_row,
    place_row,
    place_col,
    router_wide,
    gate_w,
    up_w,
    down_w,
    outgoing,
    rows,
    normed,
    hidden,
    partial,
    relay_dn,
    relay_up,
    sums_dn,
    sums_up,
    final,
    returned,
    total,
    load_sem,
    send_sem,
    rim_sem,
    src_sem,
    disp_sem,
    gat_dn,
    gat_up,
    fwd_dn,
    fwd_up,
    rel_dn,
    rel_up,
    sum_dn,
    sum_up,
    ret_sem,
):
    e = lax.axis_index("expert")
    y = lax.axis_index("hidden")
    x, z, c = lax.div(e, 16), lax.rem(lax.div(e, 2), 8), lax.rem(e, 2)
    chip = lax.div(e, 2)
    up, dn, op = lax.rem(y + 1, 4), lax.rem(y + 3, 4), lax.rem(y + 2, 4)

    def is_near(g):
        return (g == 3) | (g == 5) | (g == 7)

    def offsets(k):
        g, i = lax.div(k, BLOCKS), lax.rem(k, BLOCKS)
        dc = lax.rem(i, 2)
        third = lax.rem(i + lax.div(g + 5, 2) + 2, 3)
        hops = jnp.where((g == 0) | (g == 6), 2, jnp.where(g == 4, 4, 3))
        flip = lax.rem(dc + jnp.where((g == 2) | (g == 6), 1, 0), 2)
        far_dz = jnp.where(flip == 1, 8 - hops, hops)
        dz = jnp.where(is_near(g), jnp.where(third == 2, 7, third), far_dz)
        return lax.div(i, 2), dc, dz

    def ahead(k):
        dx, dc, dz = offsets(k)
        return (lax.rem(x + dx, 4) * 8 + lax.rem(z + dz, 8)) * 2 + lax.rem(c + dc, 2)

    def behind(k):
        dx, dc, dz = offsets(k)
        return (lax.rem(x + 4 - dx, 4) * 8 + lax.rem(z + 8 - dz, 8)) * 2 + lax.rem(c + dc, 2)

    def chip_ahead(k):
        return lax.rem(x + lax.div(k, 8), 4) * 8 + lax.rem(z + lax.rem(k, 8), 8)

    def remote(src, dst, sent, got, target):
        return pltpu.make_async_remote_copy(
            src_ref=src,
            dst_ref=dst,
            send_sem=sent,
            recv_sem=got,
            device_id=target,
            device_id_type=MESH,
        )

    def received(dst, sem):
        remote(dst, dst, send_sem.at[0], sem, (e, up)).wait_recv()

    def sent(src, sem):
        remote(src, src, sem, rim_sem.at[0], (e, up)).wait_send()

    loads = [
        pltpu.make_async_copy(source, target, load_sem.at[i])
        for i, (source, target) in enumerate(
            (
                (pixels, pixels_in),
                (table, table_in),
                (ids, ids_in),
                (router, router_in),
                (conv_weight, taps),
                (norm_gain, gain_in),
                (gate_hbm.at[0], gate_w),
                (up_hbm.at[0], up_w),
                (down_hbm.at[0], down_w),
            )
        )
    ]
    for load in loads:
        load.start()

    barrier = pltpu.get_barrier_semaphore()

    def greet(k, carry):
        target = lax.rem(e + k, EXPERTS)
        pl.semaphore_signal(barrier, inc=1, device_id=(target, y), device_id_type=MESH)
        return carry

    lax.fori_loop(1, EXPERTS, greet, 0)
    pl.semaphore_signal(barrier, inc=1, device_id=(e, up), device_id_type=MESH)
    pl.semaphore_signal(barrier, inc=1, device_id=(e, dn), device_id_type=MESH)

    padded[...] = jnp.zeros_like(padded)
    rim_wide[...] = jnp.zeros_like(rim_wide)
    conv[:, 0:SIDE] = jnp.zeros((PARTS, SIDE, OWN), BF16)
    conv[:, TOKENS - SIDE : TOKENS] = jnp.zeros((PARTS, SIDE, OWN), BF16)
    for load in loads[:6]:
        load.wait()

    def widen(i, carry):
        at = pl.multiple_of(i * SIDE, SIDE)
        padded[i + 1, LEFT : LEFT + SIDE, :] = pixels_in[pl.ds(at, SIDE), :].astype(F32)
        return carry

    lax.fori_loop(0, SIDE, widen, 0)
    near, far = LEFT, LEFT + SIDE - 1
    for half in range(2):
        lanes = slice(128 * half, 128 * half + 128)
        rim_wide[:, half, :] = padded[1, near : far + 1, lanes]
        rim_wide[:, 2 + half, :] = padded[SIDE, near : far + 1, lanes]
        rim_wide[:, 4 + half, :] = padded[1 : SIDE + 1, near, lanes]
        rim_wide[:, 6 + half, :] = padded[1 : SIDE + 1, far, lanes]
    rim_wide[:, 8, 0:8] = jnp.broadcast_to(table_in[...].astype(F32), (CHIPS, 8))
    rim_out[...] = rim_wide[...].astype(BF16)
    rim_in[c, chip] = rim_out[chip]

    def convolve(i, carry):
        mixed = padded[i + 1, near : far + 1, :]
        for a in range(3):
            for b in range(3):
                tap = taps[3 * a + b : 3 * a + b + 1, :]
                mixed = mixed + tap * padded[i + a, near - 1 + b : far + b, :]
        rounded = mixed.astype(BF16)
        conv[y, pl.ds(pl.multiple_of(i * SIDE, SIDE), SIDE), :] = rounded
        total[i] = rounded.astype(F32)
        return carry

    lax.fori_loop(0, SIDE, convolve, 0)

    pl.semaphore_wait(barrier, EXPERTS - 1 + 2)

    def send_rim(k, carry):
        target = chip_ahead(k)
        remote(
            rim_out.at[target],
            rim_in.at[c, chip],
            send_sem.at[0],
            rim_sem.at[0],
            (target * 2 + c, y),
        ).start()
        return carry

    lax.fori_loop(1, CHIPS, send_rim, 0)

    first_half, second_half = pl.ds(SIDE, INNER // 2), pl.ds(SIDE + INNER // 2, INNER // 2)
    remote(
        conv.at[y, first_half], conv.at[y, first_half], send_sem.at[12], src_sem.at[0], (e, up)
    ).start()
    remote(
        conv.at[y, second_half], conv.at[y, second_half], send_sem.at[12], src_sem.at[1], (e, dn)
    ).start()
    remote(
        conv.at[y, second_half], conv.at[y, second_half], send_sem.at[12], src_sem.at[2], (e, up)
    ).start()
    remote(
        conv.at[y, first_half], conv.at[y, first_half], send_sem.at[12], src_sem.at[3], (e, dn)
    ).start()

    onehot = (
        ids_in[...] == lax.broadcasted_iota(jnp.int32, (EXPERTS, TOKENS), 0)
    ).astype(F32)
    onehot_bf = onehot.astype(BF16)
    parts_row[...] = jnp.zeros_like(parts_row)

    def places(b, carry):
        at = pl.multiple_of(b * 256, 256)
        earlier = lax.broadcasted_iota(jnp.int32, (TOKENS, 256), 0) < (
            lax.broadcasted_iota(jnp.int32, (TOKENS, 256), 1) + at
        )
        counts = jnp.dot(
            onehot_bf, earlier.astype(F32).astype(BF16), preferred_element_type=F32
        )
        own = ids_in[0:1, pl.ds(at, 256)]
        chosen = own == lax.broadcasted_iota(jnp.int32, (EXPERTS, 256), 0)
        slot = jnp.sum(jnp.where(chosen, counts, 0.0), axis=0, keepdims=True)
        dx = (lax.shift_right_logical(own, 4) - x + 4) & 3
        dz = ((lax.shift_right_logical(own, 1) & 7) - z + 8) & 7
        dc = ((own & 1) + c) & 1
        i = dx * 2 + dc
        third = jnp.where(dz == 7, 2, dz) + 9 - i
        third = jnp.where(third >= 6, third - 6, third)
        third = jnp.where(third >= 3, third - 3, third)
        is_close = (dz <= 1) | (dz == 7)
        flip = jnp.where(dz > 4, 1, 0) ^ dc
        far_group = jnp.where(
            dz == 4, 4, jnp.where((dz == 2) | (dz == 6), 6 * flip, 1 + flip)
        )
        group = jnp.where(is_close, 3 + 2 * third, far_group)
        block = (group * BLOCKS + i).astype(F32)
        place = block * CAP + slot
        number = lax.broadcasted_iota(jnp.int32, (1, 256), 1) + at
        row, column = lax.shift_right_logical(number, 5), number & 31
        inner = (row >= 1) & (row <= SIDE - 2) & (column >= 1) & (column <= SIDE - 2)
        place_row[0:1, pl.ds(at, 256)] = jnp.where(inner, place, -1.0)
        parts_row[0:1, pl.ds(at, 256)] = block
        parts_row[1:2, pl.ds(at, 256)] = slot
        place_col[pl.ds(at, 256), :] = jnp.broadcast_to(place, (128, 256)).T
        return carry

    lax.fori_loop(0, TOKENS // 256, places, 0)

    number = lax.broadcasted_iota(jnp.int32, (1, EDGE), 1)
    along = number & 31
    edge = lax.shift_right_logical(number, 5)
    pixel = jnp.where(
        edge == 0,
        along,
        jnp.where(
            edge == 1,
            along + (TOKENS - SIDE),
            jnp.where(edge == 2, along * SIDE, along * SIDE + SIDE - 1),
        ),
    )
    picks = (lax.broadcasted_iota(jnp.int32, (TOKENS, EDGE), 0) == pixel).astype(F32).astype(BF16)
    border = jnp.dot(parts_row[...].astype(BF16), picks, preferred_element_type=F32)
    counted = (edge <= 1) | ((along >= 1) & (along <= SIDE - 2))
    place_row[0:1, TOKENS : TOKENS + EDGE] = jnp.where(
        counted, border[0:1] * CAP + border[1:2], -1.0
    )

    def widen_router(b, carry):
        at = pl.multiple_of(b * 256, 256)
        column = router_in[0:1, pl.ds(at, 256)].astype(F32)
        router_wide[pl.ds(at, 256), :] = jnp.broadcast_to(column, (128, 256)).T.astype(BF16)
        return carry

    received(rim_in.at[c, pl.ds(0, CHIPS - 1)], rim_sem.at[0])
    other = e + 1 - 2 * c
    remote(rim_in.at[c], rim_in.at[c], send_sem.at[13], rim_sem.at[2], (other, y)).start()
    held[c] = rim_in[c].astype(F32)
    received(rim_in.at[1 - c], rim_sem.at[2])
    held[1 - c] = rim_in[1 - c].astype(F32)
    tables = held[c, :, 8, :]
    tile = lax.broadcasted_iota(jnp.int32, (CHIPS, EXPERTS), 1)
    tile = ((tile & 31) * 2 + lax.shift_right_logical(tile, 5)).astype(F32)
    edges = [
        jnp.concatenate(
            [
                jnp.concatenate([held[core, :, 2 * side + half, :] for half in range(2)], axis=1)
                for core in range(2)
            ],
            axis=0,
        ).astype(BF16)
        for side in range(4)
    ]
    for direction, side in enumerate((1, 0, 3, 2, 1, 1, 0, 0)):
        chosen = (tables[:, direction : direction + 1] == tile).astype(F32).astype(BF16)
        found = jnp.dot(chosen, edges[side], preferred_element_type=F32)
        pick_wide[:, 2 * direction, :] = found[:, 0:128]
        pick_wide[:, 2 * direction + 1, :] = found[:, 128:256]
    pick_out[...] = pick_wide[...].astype(BF16)

    def send_pick(k, carry):
        target = chip_ahead(k)
        remote(
            pick_out.at[target],
            pick_in.at[chip],
            send_sem.at[1],
            rim_sem.at[1],
            (target * 2 + c, y),
        ).start()
        return carry

    lax.fori_loop(1, CHIPS, send_pick, 0)
    pick_in[chip] = pick_out[chip]

    lax.fori_loop(0, WIDTH // 256, widen_router, 0)
    received(conv.at[dn, first_half], src_sem.at[0])
    remote(
        conv.at[dn, first_half], conv.at[dn, first_half], send_sem.at[14], src_sem.at[4], (e, up)
    ).start()
    received(conv.at[up, second_half], src_sem.at[1])
    remote(
        conv.at[up, second_half], conv.at[up, second_half], send_sem.at[14], src_sem.at[5], (e, dn)
    ).start()

    received(pick_in.at[pl.ds(0, CHIPS - 1)], rim_sem.at[1])
    pick_wide[...] = pick_in[...].astype(F32)
    for half in range(2):
        lanes = slice(128 * half, 128 * half + 128)
        padded[0, near : far + 1, lanes] = pick_wide[:, half, :]
        padded[SIDE + 1, near : far + 1, lanes] = pick_wide[:, 2 + half, :]
        padded[1 : SIDE + 1, near - 1, lanes] = pick_wide[:, 4 + half, :]
        padded[1 : SIDE + 1, far + 1, lanes] = pick_wide[:, 6 + half, :]
        last = SIDE - 1
        padded[0, near - 1 : near, lanes] = pick_wide[last, 8 + half : 9 + half, :]
        padded[0, far + 1 : far + 2, lanes] = pick_wide[0, 10 + half : 11 + half, :]
        padded[SIDE + 1, near - 1 : near, lanes] = pick_wide[last, 12 + half : 13 + half, :]
        padded[SIDE + 1, far + 1 : far + 2, lanes] = pick_wide[0, 14 + half : 15 + half, :]

    def mix(center, window):
        mixed = center
        for a in range(3):
            for b in range(3):
                mixed = mixed + taps[3 * a + b : 3 * a + b + 1, :] * window(a, b)
        return mixed.astype(BF16)

    left = mix(
        padded[1 : SIDE + 1, near, :], lambda a, b: padded[a : a + SIDE, near - 1 + b, :]
    )
    right = mix(padded[1 : SIDE + 1, far, :], lambda a, b: padded[a : a + SIDE, far - 1 + b, :])
    top = mix(padded[1, near : far + 1, :], lambda a, b: padded[a, near - 1 + b : far + b, :])
    bottom = mix(
        padded[SIDE, near : far + 1, :],
        lambda a, b: padded[SIDE - 1 + a, near - 1 + b : far + b, :],
    )
    for i, strip in enumerate((top, bottom, left, right)):
        conv[y, TOKENS + i * SIDE : TOKENS + (i + 1) * SIDE, :] = strip
    total[:, 0, :] = left.astype(F32)
    total[:, SIDE - 1, :] = right.astype(F32)
    total[0] = top.astype(F32)
    total[SIDE - 1] = bottom.astype(F32)

    def blocks_of(g):
        first = lax.broadcasted_iota(jnp.int32, (ROWS, TOKENS + EDGE), 0) + g * ROWS
        return (place_row[...] == first.astype(F32)).astype(F32).astype(BF16)

    def dispatch_far(g):
        block = jnp.dot(blocks_of(g), conv[y], preferred_element_type=F32).astype(BF16)
        outgoing[y, pl.ds(g * BLOCKS, BLOCKS)] = block.reshape(BLOCKS, CAP, OWN)

        def send(k, carry):
            remote(
                outgoing.at[y, k], rows.at[y, k], send_sem.at[2], disp_sem.at[g], (ahead(k), y)
            ).start()
            return carry

        lax.fori_loop(g * BLOCKS, (g + 1) * BLOCKS, send, 0)

    def dispatch_near(g):
        chosen = blocks_of(g)
        for part in range(PARTS):
            block = jnp.dot(chosen, conv[part], preferred_element_type=F32).astype(BF16)
            outgoing[part, pl.ds(g * BLOCKS, BLOCKS)] = block.reshape(BLOCKS, CAP, OWN)

        @pl.when(g == 3)
        def _():
            pltpu.make_async_copy(
                outgoing.at[:, OWN_BLOCK], rows.at[:, OWN_BLOCK], disp_sem.at[3]
            ).start()

        def send(k, carry):
            remote(
                outgoing.at[:, k], rows.at[:, k], send_sem.at[15], disp_sem.at[g], (ahead(k), y)
            ).start()
            return carry

        lax.fori_loop(g * BLOCKS + jnp.where(g == 3, 1, 0), (g + 1) * BLOCKS, send, 0)

    pack = pl.ds(TOKENS, EDGE)
    pack_low, pack_high = pl.ds(TOKENS, EDGE // 2), pl.ds(TOKENS + EDGE // 2, EDGE // 2)

    def forward_pack():
        received(conv.at[dn, pack], src_sem.at[6])
        remote(
            conv.at[dn, pack_low], conv.at[dn, pack_low], send_sem.at[17], src_sem.at[8], (e, up)
        ).start()
        received(conv.at[up, pack], src_sem.at[7])
        remote(
            conv.at[up, pack_high], conv.at[up, pack_high], send_sem.at[17], src_sem.at[9], (e, dn)
        ).start()

    def conv_complete():
        received(conv.at[dn, second_half], src_sem.at[2])
        received(conv.at[up, first_half], src_sem.at[3])
        received(conv.at[op, first_half], src_sem.at[4])
        received(conv.at[op, second_half], src_sem.at[5])
        received(conv.at[op, pack_low], src_sem.at[8])
        received(conv.at[op, pack_high], src_sem.at[9])

    def gather(g):
        span = pl.ds(g * BLOCKS, BLOCKS)
        mine = rows.at[y, span]
        received(mine, disp_sem.at[g])
        remote(mine, mine, send_sem.at[3], gat_dn.at[g], (e, up)).start()
        remote(mine, mine, send_sem.at[4], gat_up.at[g], (e, dn)).start()

        @pl.when(g == 0)
        def _():
            remote(mine, mine, send_sem.at[18], fwd_dn.at[0], (e, op)).start()

    def forward(g):
        received(rows.at[dn, pl.ds(g * BLOCKS, BLOCKS)], gat_dn.at[g])

        @pl.when(g > 0)
        def _():
            low = rows.at[dn, pl.ds(g * BLOCKS, HALF)]
            remote(low, low, send_sem.at[5], fwd_dn.at[g], (e, up)).start()

        received(rows.at[up, pl.ds(g * BLOCKS, BLOCKS)], gat_up.at[g])

        @pl.when(g > 0)
        def _():
            high = rows.at[up, pl.ds(g * BLOCKS + HALF, HALF)]
            remote(high, high, send_sem.at[6], fwd_up.at[g], (e, dn)).start()

    def arrived(g):
        @pl.when(g == 0)
        def _():
            received(rows.at[op, pl.ds(g * BLOCKS, BLOCKS)], fwd_dn.at[g])

        @pl.when(g > 0)
        def _():
            received(rows.at[op, pl.ds(g * BLOCKS, HALF)], fwd_dn.at[g])
            received(rows.at[op, pl.ds(g * BLOCKS + HALF, HALF)], fwd_up.at[g])

    def expert(g):
        span = pl.ds(g * BLOCKS, BLOCKS)
        pl.when(is_near(g))(lambda: received(rows.at[:, span], disp_sem.at[g]))
        pl.when(jnp.logical_not(is_near(g)))(lambda: arrived(g))
        squares = jnp.zeros((ROWS, 1), F32)
        for part in range(PARTS):
            wide = rows[part, span].reshape(ROWS, OWN).astype(F32)
            squares = squares + jnp.sum(wide * wide, axis=1, keepdims=True)
        scale = lax.rsqrt(squares * (1.0 / WIDTH) + EPSILON)
        for part in range(PARTS):
            wide = rows[part, span].reshape(ROWS, OWN).astype(F32)
            normed[:, part * OWN : (part + 1) * OWN] = (
                wide * scale * gain_in[0:1, part * OWN : (part + 1) * OWN]
            ).astype(BF16)
        score = jnp.dot(normed[...], router_wide[...], preferred_element_type=F32)
        weight = 1.0 / (1.0 + jnp.exp(-score))
        weight = jnp.concatenate([weight, weight], axis=1)

        def units(n, carry):
            at = pl.ds(pl.multiple_of(n * 256, 256), 256)
            gate = jnp.dot(normed[...], gate_w[:, at], preferred_element_type=F32)
            lift = jnp.dot(normed[...], up_w[:, at], preferred_element_type=F32)
            hidden[:, at] = (gate / (1.0 + jnp.exp(-gate)) * lift * weight).astype(BF16)
            return carry

        lax.fori_loop(0, UNITS // 256, units, 0)

        def channels(part):
            at = pl.ds(pl.multiple_of(part * OWN, OWN), OWN)
            result = jnp.dot(hidden[...], down_w[:, at], preferred_element_type=F32)
            partial[part, span] = result.astype(BF16).reshape(BLOCKS, CAP, OWN)

        low, high = pl.ds(g * BLOCKS, HALF), pl.ds(g * BLOCKS + HALF, HALF)
        slot = pl.ds(g * HALF, HALF)
        channels(op)
        remote(
            partial.at[op, low], relay_dn.at[slot], send_sem.at[7], rel_dn.at[g], (e, up)
        ).start()
        remote(
            partial.at[op, high], relay_up.at[slot], send_sem.at[8], rel_up.at[g], (e, dn)
        ).start()
        channels(up)
        remote(
            partial.at[up, high], sums_dn.at[high], send_sem.at[9], sum_dn.at[g], (e, up)
        ).start()
        channels(dn)
        remote(
            partial.at[dn, low], sums_up.at[low], send_sem.at[10], sum_up.at[g], (e, dn)
        ).start()
        channels(y)

    def relay(g):
        low, high = pl.ds(g * BLOCKS, HALF), pl.ds(g * BLOCKS + HALF, HALF)
        slot = pl.ds(g * HALF, HALF)
        received(relay_dn.at[slot], rel_dn.at[g])
        partial[up, low] = (partial[up, low].astype(F32) + relay_dn[slot].astype(F32)).astype(BF16)
        remote(
            partial.at[up, low], sums_dn.at[low], send_sem.at[9], sum_dn.at[g], (e, up)
        ).start()
        received(relay_up.at[slot], rel_up.at[g])
        partial[dn, high] = (
            partial[dn, high].astype(F32) + relay_up[slot].astype(F32)
        ).astype(BF16)
        remote(
            partial.at[dn, high], sums_up.at[high], send_sem.at[10], sum_up.at[g], (e, dn)
        ).start()

    def give_back(g):
        span = pl.ds(g * BLOCKS, BLOCKS)
        received(sums_dn.at[span], sum_dn.at[g])
        received(sums_up.at[span], sum_up.at[g])
        final[span] = (
            partial[y, span].astype(F32) + sums_dn[span].astype(F32) + sums_up[span].astype(F32)
        ).astype(BF16)

        @pl.when(g == 3)
        def _():
            pltpu.make_async_copy(
                final.at[OWN_BLOCK], returned.at[OWN_BLOCK], ret_sem.at[3]
            ).start()

        def send(k, carry):
            remote(
                final.at[k], returned.at[k], send_sem.at[11], ret_sem.at[g], (behind(k), y)
            ).start()
            return carry

        lax.fori_loop(g * BLOCKS + jnp.where(g == 3, 1, 0), (g + 1) * BLOCKS, send, 0)

    def combine(g):
        span = pl.ds(g * BLOCKS, BLOCKS)
        received(returned.at[span], ret_sem.at[g])
        block = returned[span].reshape(ROWS, OWN)
        number = (lax.broadcasted_iota(jnp.int32, (256, 128), 1) + g * ROWS).astype(F32)

        def add(b, carry):
            at = pl.ds(pl.multiple_of(b * 256, 256), 256)
            place = place_col[at, :]
            chosen = jnp.concatenate(
                [(place == number).astype(F32), (place == number + 128.0).astype(F32)], axis=1
            ).astype(BF16)
            tile_rows = pl.ds(b * 8, 8)
            added = jnp.dot(chosen, block, preferred_element_type=F32)
            total[tile_rows] += added.reshape(8, SIDE, OWN)
            return carry

        lax.fori_loop(0, TOKENS // 256, add, 0)

    dispatch_far(0)
    remote(conv.at[y, pack], conv.at[y, pack], send_sem.at[16], src_sem.at[6], (e, up)).start()
    remote(conv.at[y, pack], conv.at[y, pack], send_sem.at[16], src_sem.at[7], (e, dn)).start()
    dispatch_far(1)
    dispatch_far(2)
    forward_pack()
    for load in loads[6:]:
        load.wait()

    def step(s, carry):
        pl.when((s < GROUPS) & jnp.logical_not(is_near(s)))(
            lambda: gather(s)
        )
        pl.when((s >= 1) & (s < GROUPS + 1) & jnp.logical_not(is_near(s - 1)))(
            lambda: forward(s - 1)
        )
        pl.when(s == 0)(conv_complete)
        pl.when((s >= 2) & (s < GROUPS + 2))(lambda: expert(s - 2))
        pl.when((s >= 3) & (s < GROUPS + 3))(lambda: relay(s - 3))
        pl.when((s >= 6) & (s < GROUPS + 6))(lambda: combine(s - 6))
        pl.when((s >= 4) & (s < GROUPS + 4))(lambda: give_back(s - 4))
        pl.when((s + 3 < GROUPS) & is_near(s + 3))(lambda: dispatch_near(s + 3))
        pl.when((s + 3 < GROUPS) & jnp.logical_not(is_near(s + 3)))(lambda: dispatch_far(s + 3))
        return carry

    lax.fori_loop(0, GROUPS + 6, step, 0)
    out[...] = total[...].reshape(TOKENS, OWN).astype(BF16)

    def span_of(count):
        return outgoing.at[0, pl.ds(0, count)]

    sent(rim_out.at[pl.ds(0, CHIPS - 1)], send_sem.at[0])
    sent(pick_out.at[pl.ds(0, CHIPS - 1)], send_sem.at[1])
    sent(rim_in.at[0], send_sem.at[13])
    sent(span_of(40), send_sem.at[2])
    sent(span_of(40), send_sem.at[3])
    sent(span_of(40), send_sem.at[4])
    sent(span_of(16), send_sem.at[5])
    sent(span_of(16), send_sem.at[6])
    sent(span_of(8), send_sem.at[18])
    sent(span_of(32), send_sem.at[7])
    sent(span_of(32), send_sem.at[8])
    sent(span_of(64), send_sem.at[9])
    sent(span_of(64), send_sem.at[10])
    sent(span_of(63), send_sem.at[11])
    sent(conv.at[pl.ds(0, 2), pl.ds(0, INNER)], send_sem.at[12])
    sent(conv.at[0, pl.ds(0, INNER)], send_sem.at[14])
    sent(outgoing.at[:, pl.ds(0, 23)], send_sem.at[15])
    sent(conv.at[0, pl.ds(0, 2 * EDGE)], send_sem.at[16])
    sent(conv.at[0, pl.ds(0, EDGE)], send_sem.at[17])


def shards(
    pixels,
    conv_weight,
    norm_gain,
    router_weight,
    gate_weight,
    up_weight,
    down_weight,
    expert_ids,
    neighbours,
):
    vmem = pl.BlockSpec(memory_space=pltpu.VMEM)
    hbm = pl.BlockSpec(memory_space=pltpu.HBM)
    blocks = (EXPERTS, CAP, OWN)
    per_group = pltpu.SemaphoreType.DMA((GROUPS,))
    return pl.pallas_call(
        kernel,
        out_shape=jax.ShapeDtypeStruct((TOKENS, OWN), BF16),
        in_specs=[hbm] * 9,
        out_specs=vmem,
        scratch_shapes=[
            pltpu.VMEM((TOKENS, OWN), BF16),
            pltpu.VMEM((9, OWN), F32),
            pltpu.VMEM((1, WIDTH), F32),
            pltpu.VMEM((1, WIDTH), BF16),
            pltpu.VMEM((1, TOKENS), jnp.int32),
            pltpu.VMEM((1, 8), jnp.int32),
            pltpu.VMEM((SIDE + 2, SIDE + 2 * LEFT, OWN), F32),
            pltpu.VMEM((CHIPS, 16, 128), F32),
            pltpu.VMEM((CHIPS, 16, 128), BF16),
            pltpu.VMEM((2, CHIPS, 16, 128), BF16),
            pltpu.VMEM((2, CHIPS, 16, 128), F32),
            pltpu.VMEM((CHIPS, 16, 128), F32),
            pltpu.VMEM((CHIPS, 16, 128), BF16),
            pltpu.VMEM((CHIPS, 16, 128), BF16),
            pltpu.VMEM((PARTS, TOKENS + EDGE, OWN), BF16),
            pltpu.VMEM((8, TOKENS), F32),
            pltpu.VMEM((1, TOKENS + EDGE), F32),
            pltpu.VMEM((TOKENS, 128), F32),
            pltpu.VMEM((WIDTH, 128), BF16),
            pltpu.VMEM((WIDTH, UNITS), BF16),
            pltpu.VMEM((WIDTH, UNITS), BF16),
            pltpu.VMEM((UNITS, WIDTH), BF16),
            pltpu.VMEM((PARTS,) + blocks, BF16),
            pltpu.VMEM((PARTS,) + blocks, BF16),
            pltpu.VMEM((ROWS, WIDTH), BF16),
            pltpu.VMEM((ROWS, UNITS), BF16),
            pltpu.VMEM((PARTS,) + blocks, BF16),
            pltpu.VMEM((EXPERTS // 2, CAP, OWN), BF16),
            pltpu.VMEM((EXPERTS // 2, CAP, OWN), BF16),
            pltpu.VMEM(blocks, BF16),
            pltpu.VMEM(blocks, BF16),
            pltpu.VMEM(blocks, BF16),
            pltpu.VMEM(blocks, BF16),
            pltpu.VMEM((SIDE, SIDE, OWN), F32),
            pltpu.SemaphoreType.DMA((9,)),
            pltpu.SemaphoreType.DMA((19,)),
            pltpu.SemaphoreType.DMA((3,)),
            pltpu.SemaphoreType.DMA((10,)),
        ]
        + [per_group] * 10,
        compiler_params=pltpu.CompilerParams(
            collective_id=0, has_side_effects=True, vmem_limit_bytes=63 * 1024 * 1024
        ),
    )(
        pixels,
        conv_weight,
        norm_gain.reshape(1, WIDTH),
        router_weight.reshape(1, WIDTH),
        expert_ids.reshape(1, TOKENS),
        neighbours,
        gate_weight,
        up_weight,
        down_weight,
    )


def solution(mesh):
    in_specs = (
        P("expert", "hidden"),
        P(None, "hidden"),
        P(),
        P(None, "expert"),
        P("expert", None, "hidden"),
        P("expert", None, "hidden"),
        P("expert", "hidden", None),
        P("expert", None),
        P("expert", None),
    )
    out_specs = P("expert", "hidden")
    return jax.shard_map(shards, mesh=mesh, in_specs=in_specs, out_specs=out_specs, check_vma=False)
```

```python
import jax
import jax.numpy as jnp
from jax import lax
from jax.experimental import pallas as pl
from jax.experimental.pallas import tpu as pltpu
from jax.sharding import PartitionSpec as P

MESH = pl.DeviceIdType.MESH
F32 = jnp.float32
BF16 = jnp.bfloat16

SIDE = 32
TOKENS = SIDE * SIDE
EXPERTS = 64
CAP = 32
OWN = 256
PARTS = 4
UNITS = 1024
WIDTH = OWN * PARTS
GROUPS = 8
BLOCKS = EXPERTS // GROUPS
HALF = BLOCKS // 2
ROWS = BLOCKS * CAP
CHIPS = EXPERTS // 2
EDGE = 4 * SIDE
INNER = TOKENS - 2 * SIDE
OWN_BLOCK = 24
LEFT = 8
EPSILON = 1e-05


def kernel(
    pixels,
    conv_weight,
    norm_gain,
    router,
    ids,
    table,
    gate_hbm,
    up_hbm,
    down_hbm,
    out,
    pixels_in,
    taps,
    gain_in,
    router_in,
    ids_in,
    table_in,
    padded,
    rim_wide,
    rim_out,
    rim_in,
    held,
    pick_wide,
    pick_out,
    pick_in,
    conv,
    parts_row,
    place_row,
    place_col,
    router_wide,
    gate_w,
    up_w,
    down_w,
    outgoing,
    rows,
    normed,
    hidden,
    partial,
    relay_dn,
    relay_up,
    sums_dn,
    sums_up,
    final,
    returned,
    total,
    load_sem,
    send_sem,
    rim_sem,
    src_sem,
    disp_sem,
    gat_dn,
    gat_up,
    fwd_dn,
    fwd_up,
    rel_dn,
    rel_up,
    sum_dn,
    sum_up,
    ret_sem,
):
    e = lax.axis_index("expert")
    y = lax.axis_index("hidden")
    x, z, c = lax.div(e, 16), lax.rem(lax.div(e, 2), 8), lax.rem(e, 2)
    chip = lax.div(e, 2)
    up, dn, op = lax.rem(y + 1, 4), lax.rem(y + 3, 4), lax.rem(y + 2, 4)

    def is_near(g):
        return (g == 3) | (g == 5) | (g == 7)

    def offsets(k):
        g, i = lax.div(k, BLOCKS), lax.rem(k, BLOCKS)
        dc = lax.rem(i, 2)
        third = lax.rem(i + lax.div(g + 5, 2) + 2, 3)
        hops = jnp.where((g == 0) | (g == 6), 2, jnp.where(g == 4, 4, 3))
        flip = lax.rem(dc + jnp.where((g == 2) | (g == 6), 1, 0), 2)
        far_dz = jnp.where(flip == 1, 8 - hops, hops)
        dz = jnp.where(is_near(g), jnp.where(third == 2, 7, third), far_dz)
        return lax.div(i, 2), dc, dz

    def ahead(k):
        dx, dc, dz = offsets(k)
        return (lax.rem(x + dx, 4) * 8 + lax.rem(z + dz, 8)) * 2 + lax.rem(c + dc, 2)

    def behind(k):
        dx, dc, dz = offsets(k)
        return (lax.rem(x + 4 - dx, 4) * 8 + lax.rem(z + 8 - dz, 8)) * 2 + lax.rem(c + dc, 2)

    def chip_ahead(k):
        return lax.rem(x + lax.div(k, 8), 4) * 8 + lax.rem(z + lax.rem(k, 8), 8)

    def remote(src, dst, sent, got, target):
        return pltpu.make_async_remote_copy(
            src_ref=src,
            dst_ref=dst,
            send_sem=sent,
            recv_sem=got,
            device_id=target,
            device_id_type=MESH,
        )

    def received(dst, sem):
        remote(dst, dst, send_sem.at[0], sem, (e, up)).wait_recv()

    def sent(src, sem):
        remote(src, src, sem, rim_sem.at[0], (e, up)).wait_send()

    loads = [
        pltpu.make_async_copy(source, target, load_sem.at[i])
        for i, (source, target) in enumerate(
            (
                (pixels, pixels_in),
                (table, table_in),
                (ids, ids_in),
                (router, router_in),
                (conv_weight, taps),
                (norm_gain, gain_in),
                (gate_hbm.at[0], gate_w),
                (up_hbm.at[0], up_w),
                (down_hbm.at[0], down_w),
            )
        )
    ]
    for load in loads:
        load.start()

    barrier = pltpu.get_barrier_semaphore()

    def greet(k, carry):
        target = lax.rem(e + k, EXPERTS)
        pl.semaphore_signal(barrier, inc=1, device_id=(target, y), device_id_type=MESH)
        return carry

    lax.fori_loop(1, EXPERTS, greet, 0)
    pl.semaphore_signal(barrier, inc=1, device_id=(e, up), device_id_type=MESH)
    pl.semaphore_signal(barrier, inc=1, device_id=(e, dn), device_id_type=MESH)

    padded[...] = jnp.zeros_like(padded)
    rim_wide[...] = jnp.zeros_like(rim_wide)
    conv[:, 0:SIDE] = jnp.zeros((PARTS, SIDE, OWN), BF16)
    conv[:, TOKENS - SIDE : TOKENS] = jnp.zeros((PARTS, SIDE, OWN), BF16)
    for load in loads[:6]:
        load.wait()

    def widen(i, carry):
        at = pl.multiple_of(i * SIDE, SIDE)
        padded[i + 1, LEFT : LEFT + SIDE, :] = pixels_in[pl.ds(at, SIDE), :].astype(F32)
        return carry

    lax.fori_loop(0, SIDE, widen, 0)
    near, far = LEFT, LEFT + SIDE - 1
    for half in range(2):
        lanes = slice(128 * half, 128 * half + 128)
        rim_wide[:, half, :] = padded[1, near : far + 1, lanes]
        rim_wide[:, 2 + half, :] = padded[SIDE, near : far + 1, lanes]
        rim_wide[:, 4 + half, :] = padded[1 : SIDE + 1, near, lanes]
        rim_wide[:, 6 + half, :] = padded[1 : SIDE + 1, far, lanes]
    rim_wide[:, 8, 0:8] = jnp.broadcast_to(table_in[...].astype(F32), (CHIPS, 8))
    rim_out[...] = rim_wide[...].astype(BF16)
    rim_in[c, chip] = rim_out[chip]

    def convolve(i, carry):
        mixed = padded[i + 1, near : far + 1, :]
        for a in range(3):
            for b in range(3):
                tap = taps[3 * a + b : 3 * a + b + 1, :]
                mixed = mixed + tap * padded[i + a, near - 1 + b : far + b, :]
        rounded = mixed.astype(BF16)
        conv[y, pl.ds(pl.multiple_of(i * SIDE, SIDE), SIDE), :] = rounded
        total[i] = rounded.astype(F32)
        return carry

    lax.fori_loop(0, SIDE, convolve, 0)

    pl.semaphore_wait(barrier, EXPERTS - 1 + 2)

    def send_rim(k, carry):
        target = chip_ahead(k)
        remote(
            rim_out.at[target],
            rim_in.at[c, chip],
            send_sem.at[0],
            rim_sem.at[0],
            (target * 2 + c, y),
        ).start()
        return carry

    lax.fori_loop(1, CHIPS, send_rim, 0)

    first_half, second_half = pl.ds(SIDE, INNER // 2), pl.ds(SIDE + INNER // 2, INNER // 2)
    remote(
        conv.at[y, first_half], conv.at[y, first_half], send_sem.at[12], src_sem.at[0], (e, up)
    ).start()
    remote(
        conv.at[y, second_half], conv.at[y, second_half], send_sem.at[12], src_sem.at[1], (e, dn)
    ).start()
    remote(
        conv.at[y, second_half], conv.at[y, second_half], send_sem.at[12], src_sem.at[2], (e, up)
    ).start()
    remote(
        conv.at[y, first_half], conv.at[y, first_half], send_sem.at[12], src_sem.at[3], (e, dn)
    ).start()

    onehot = (
        ids_in[...] == lax.broadcasted_iota(jnp.int32, (EXPERTS, TOKENS), 0)
    ).astype(F32)
    onehot_bf = onehot.astype(BF16)
    parts_row[...] = jnp.zeros_like(parts_row)

    def places(b, carry):
        at = pl.multiple_of(b * 256, 256)
        earlier = lax.broadcasted_iota(jnp.int32, (TOKENS, 256), 0) < (
            lax.broadcasted_iota(jnp.int32, (TOKENS, 256), 1) + at
        )
        counts = jnp.dot(
            onehot_bf, earlier.astype(F32).astype(BF16), preferred_element_type=F32
        )
        own = ids_in[0:1, pl.ds(at, 256)]
        chosen = own == lax.broadcasted_iota(jnp.int32, (EXPERTS, 256), 0)
        slot = jnp.sum(jnp.where(chosen, counts, 0.0), axis=0, keepdims=True)
        dx = (lax.shift_right_logical(own, 4) - x + 4) & 3
        dz = ((lax.shift_right_logical(own, 1) & 7) - z + 8) & 7
        dc = ((own & 1) + c) & 1
        i = dx * 2 + dc
        third = jnp.where(dz == 7, 2, dz) + 9 - i
        third = jnp.where(third >= 6, third - 6, third)
        third = jnp.where(third >= 3, third - 3, third)
        is_close = (dz <= 1) | (dz == 7)
        flip = jnp.where(dz > 4, 1, 0) ^ dc
        far_group = jnp.where(
            dz == 4, 4, jnp.where((dz == 2) | (dz == 6), 6 * flip, 1 + flip)
        )
        group = jnp.where(is_close, 3 + 2 * third, far_group)
        block = (group * BLOCKS + i).astype(F32)
        place = block * CAP + slot
        number = lax.broadcasted_iota(jnp.int32, (1, 256), 1) + at
        row, column = lax.shift_right_logical(number, 5), number & 31
        inner = (row >= 1) & (row <= SIDE - 2) & (column >= 1) & (column <= SIDE - 2)
        place_row[0:1, pl.ds(at, 256)] = jnp.where(inner, place, -1.0)
        parts_row[0:1, pl.ds(at, 256)] = block
        parts_row[1:2, pl.ds(at, 256)] = slot
        place_col[pl.ds(at, 256), :] = jnp.broadcast_to(place, (128, 256)).T
        return carry

    lax.fori_loop(0, TOKENS // 256, places, 0)

    number = lax.broadcasted_iota(jnp.int32, (1, EDGE), 1)
    along = number & 31
    edge = lax.shift_right_logical(number, 5)
    pixel = jnp.where(
        edge == 0,
        along,
        jnp.where(
            edge == 1,
            along + (TOKENS - SIDE),
            jnp.where(edge == 2, along * SIDE, along * SIDE + SIDE - 1),
        ),
    )
    picks = (lax.broadcasted_iota(jnp.int32, (TOKENS, EDGE), 0) == pixel).astype(F32).astype(BF16)
    border = jnp.dot(parts_row[...].astype(BF16), picks, preferred_element_type=F32)
    counted = (edge <= 1) | ((along >= 1) & (along <= SIDE - 2))
    place_row[0:1, TOKENS : TOKENS + EDGE] = jnp.where(
        counted, border[0:1] * CAP + border[1:2], -1.0
    )

    def widen_router(b, carry):
        at = pl.multiple_of(b * 256, 256)
        column = router_in[0:1, pl.ds(at, 256)].astype(F32)
        router_wide[pl.ds(at, 256), :] = jnp.broadcast_to(column, (128, 256)).T.astype(BF16)
        return carry

    received(rim_in.at[c, pl.ds(0, CHIPS - 1)], rim_sem.at[0])
    other = e + 1 - 2 * c
    remote(rim_in.at[c], rim_in.at[c], send_sem.at[13], rim_sem.at[2], (other, y)).start()
    held[c] = rim_in[c].astype(F32)
    received(rim_in.at[1 - c], rim_sem.at[2])
    held[1 - c] = rim_in[1 - c].astype(F32)
    tables = held[c, :, 8, :]
    tile = lax.broadcasted_iota(jnp.int32, (CHIPS, EXPERTS), 1)
    tile = ((tile & 31) * 2 + lax.shift_right_logical(tile, 5)).astype(F32)
    edges = [
        jnp.concatenate(
            [
                jnp.concatenate([held[core, :, 2 * side + half, :] for half in range(2)], axis=1)
                for core in range(2)
            ],
            axis=0,
        ).astype(BF16)
        for side in range(4)
    ]
    for direction, side in enumerate((1, 0, 3, 2, 1, 1, 0, 0)):
        chosen = (tables[:, direction : direction + 1] == tile).astype(F32).astype(BF16)
        found = jnp.dot(chosen, edges[side], preferred_element_type=F32)
        pick_wide[:, 2 * direction, :] = found[:, 0:128]
        pick_wide[:, 2 * direction + 1, :] = found[:, 128:256]
    pick_out[...] = pick_wide[...].astype(BF16)

    def send_pick(k, carry):
        target = chip_ahead(k)
        remote(
            pick_out.at[target],
            pick_in.at[chip],
            send_sem.at[1],
            rim_sem.at[1],
            (target * 2 + c, y),
        ).start()
        return carry

    lax.fori_loop(1, CHIPS, send_pick, 0)
    pick_in[chip] = pick_out[chip]

    lax.fori_loop(0, WIDTH // 256, widen_router, 0)
    received(conv.at[dn, first_half], src_sem.at[0])
    remote(
        conv.at[dn, first_half], conv.at[dn, first_half], send_sem.at[14], src_sem.at[4], (e, up)
    ).start()
    received(conv.at[up, second_half], src_sem.at[1])
    remote(
        conv.at[up, second_half], conv.at[up, second_half], send_sem.at[14], src_sem.at[5], (e, dn)
    ).start()

    received(pick_in.at[pl.ds(0, CHIPS - 1)], rim_sem.at[1])
    pick_wide[...] = pick_in[...].astype(F32)
    for half in range(2):
        lanes = slice(128 * half, 128 * half + 128)
        padded[0, near : far + 1, lanes] = pick_wide[:, half, :]
        padded[SIDE + 1, near : far + 1, lanes] = pick_wide[:, 2 + half, :]
        padded[1 : SIDE + 1, near - 1, lanes] = pick_wide[:, 4 + half, :]
        padded[1 : SIDE + 1, far + 1, lanes] = pick_wide[:, 6 + half, :]
        last = SIDE - 1
        padded[0, near - 1 : near, lanes] = pick_wide[last, 8 + half : 9 + half, :]
        padded[0, far + 1 : far + 2, lanes] = pick_wide[0, 10 + half : 11 + half, :]
        padded[SIDE + 1, near - 1 : near, lanes] = pick_wide[last, 12 + half : 13 + half, :]
        padded[SIDE + 1, far + 1 : far + 2, lanes] = pick_wide[0, 14 + half : 15 + half, :]

    def mix(center, window):
        mixed = center
        for a in range(3):
            for b in range(3):
                mixed = mixed + taps[3 * a + b : 3 * a + b + 1, :] * window(a, b)
        return mixed.astype(BF16)

    left = mix(
        padded[1 : SIDE + 1, near, :], lambda a, b: padded[a : a + SIDE, near - 1 + b, :]
    )
    right = mix(padded[1 : SIDE + 1, far, :], lambda a, b: padded[a : a + SIDE, far - 1 + b, :])
    top = mix(padded[1, near : far + 1, :], lambda a, b: padded[a, near - 1 + b : far + b, :])
    bottom = mix(
        padded[SIDE, near : far + 1, :],
        lambda a, b: padded[SIDE - 1 + a, near - 1 + b : far + b, :],
    )
    for i, strip in enumerate((top, bottom, left, right)):
        conv[y, TOKENS + i * SIDE : TOKENS + (i + 1) * SIDE, :] = strip
    total[:, 0, :] = left.astype(F32)
    total[:, SIDE - 1, :] = right.astype(F32)
    total[0] = top.astype(F32)
    total[SIDE - 1] = bottom.astype(F32)

    def blocks_of(g):
        first = lax.broadcasted_iota(jnp.int32, (ROWS, TOKENS + EDGE), 0) + g * ROWS
        return (place_row[...] == first.astype(F32)).astype(F32).astype(BF16)

    def dispatch_far(g):
        block = jnp.dot(blocks_of(g), conv[y], preferred_element_type=F32).astype(BF16)
        outgoing[y, pl.ds(g * BLOCKS, BLOCKS)] = block.reshape(BLOCKS, CAP, OWN)

        def send(k, carry):
            remote(
                outgoing.at[y, k], rows.at[y, k], send_sem.at[2], disp_sem.at[g], (ahead(k), y)
            ).start()
            return carry

        lax.fori_loop(g * BLOCKS, (g + 1) * BLOCKS, send, 0)

    def dispatch_near(g):
        chosen = blocks_of(g)
        for part in range(PARTS):
            block = jnp.dot(chosen, conv[part], preferred_element_type=F32).astype(BF16)
            outgoing[part, pl.ds(g * BLOCKS, BLOCKS)] = block.reshape(BLOCKS, CAP, OWN)

        @pl.when(g == 3)
        def _():
            pltpu.make_async_copy(
                outgoing.at[:, OWN_BLOCK], rows.at[:, OWN_BLOCK], disp_sem.at[3]
            ).start()

        def send(k, carry):
            remote(
                outgoing.at[:, k], rows.at[:, k], send_sem.at[15], disp_sem.at[g], (ahead(k), y)
            ).start()
            return carry

        lax.fori_loop(g * BLOCKS + jnp.where(g == 3, 1, 0), (g + 1) * BLOCKS, send, 0)

    pack = pl.ds(TOKENS, EDGE)
    pack_low, pack_high = pl.ds(TOKENS, EDGE // 2), pl.ds(TOKENS + EDGE // 2, EDGE // 2)

    def forward_pack():
        received(conv.at[dn, pack], src_sem.at[6])
        remote(
            conv.at[dn, pack_low], conv.at[dn, pack_low], send_sem.at[17], src_sem.at[8], (e, up)
        ).start()
        received(conv.at[up, pack], src_sem.at[7])
        remote(
            conv.at[up, pack_high], conv.at[up, pack_high], send_sem.at[17], src_sem.at[9], (e, dn)
        ).start()

    def conv_complete():
        received(conv.at[dn, second_half], src_sem.at[2])
        received(conv.at[up, first_half], src_sem.at[3])
        received(conv.at[op, first_half], src_sem.at[4])
        received(conv.at[op, second_half], src_sem.at[5])
        received(conv.at[op, pack_low], src_sem.at[8])
        received(conv.at[op, pack_high], src_sem.at[9])

    def gather(g):
        span = pl.ds(g * BLOCKS, BLOCKS)
        mine = rows.at[y, span]
        received(mine, disp_sem.at[g])
        remote(mine, mine, send_sem.at[3], gat_dn.at[g], (e, up)).start()
        remote(mine, mine, send_sem.at[4], gat_up.at[g], (e, dn)).start()

        @pl.when(g == 0)
        def _():
            remote(mine, mine, send_sem.at[18], fwd_dn.at[0], (e, op)).start()

    def forward(g):
        received(rows.at[dn, pl.ds(g * BLOCKS, BLOCKS)], gat_dn.at[g])

        @pl.when(g > 0)
        def _():
            low = rows.at[dn, pl.ds(g * BLOCKS, HALF)]
            remote(low, low, send_sem.at[5], fwd_dn.at[g], (e, up)).start()

        received(rows.at[up, pl.ds(g * BLOCKS, BLOCKS)], gat_up.at[g])

        @pl.when(g > 0)
        def _():
            high = rows.at[up, pl.ds(g * BLOCKS + HALF, HALF)]
            remote(high, high, send_sem.at[6], fwd_up.at[g], (e, dn)).start()

    def arrived(g):
        @pl.when(g == 0)
        def _():
            received(rows.at[op, pl.ds(g * BLOCKS, BLOCKS)], fwd_dn.at[g])

        @pl.when(g > 0)
        def _():
            received(rows.at[op, pl.ds(g * BLOCKS, HALF)], fwd_dn.at[g])
            received(rows.at[op, pl.ds(g * BLOCKS + HALF, HALF)], fwd_up.at[g])

    def expert(g):
        span = pl.ds(g * BLOCKS, BLOCKS)
        pl.when(is_near(g))(lambda: received(rows.at[:, span], disp_sem.at[g]))
        pl.when(jnp.logical_not(is_near(g)))(lambda: arrived(g))
        squares = jnp.zeros((ROWS, 1), F32)
        for part in range(PARTS):
            wide = rows[part, span].reshape(ROWS, OWN).astype(F32)
            squares = squares + jnp.sum(wide * wide, axis=1, keepdims=True)
        scale = lax.rsqrt(squares * (1.0 / WIDTH) + EPSILON)
        for part in range(PARTS):
            wide = rows[part, span].reshape(ROWS, OWN).astype(F32)
            normed[:, part * OWN : (part + 1) * OWN] = (
                wide * scale * gain_in[0:1, part * OWN : (part + 1) * OWN]
            ).astype(BF16)
        score = jnp.dot(normed[...], router_wide[...], preferred_element_type=F32)
        weight = 1.0 / (1.0 + jnp.exp(-score))
        weight = jnp.concatenate([weight, weight], axis=1)

        def units(n, carry):
            at = pl.ds(pl.multiple_of(n * 256, 256), 256)
            gate = jnp.dot(normed[...], gate_w[:, at], preferred_element_type=F32)
            lift = jnp.dot(normed[...], up_w[:, at], preferred_element_type=F32)
            hidden[:, at] = (gate / (1.0 + jnp.exp(-gate)) * lift * weight).astype(BF16)
            return carry

        lax.fori_loop(0, UNITS // 256, units, 0)

        def channels(part):
            at = pl.ds(pl.multiple_of(part * OWN, OWN), OWN)
            result = jnp.dot(hidden[...], down_w[:, at], preferred_element_type=F32)
            partial[part, span] = result.astype(BF16).reshape(BLOCKS, CAP, OWN)

        low, high = pl.ds(g * BLOCKS, HALF), pl.ds(g * BLOCKS + HALF, HALF)
        slot = pl.ds(g * HALF, HALF)
        channels(op)
        remote(
            partial.at[op, low], relay_dn.at[slot], send_sem.at[7], rel_dn.at[g], (e, up)
        ).start()
        remote(
            partial.at[op, high], relay_up.at[slot], send_sem.at[8], rel_up.at[g], (e, dn)
        ).start()
        channels(up)
        remote(
            partial.at[up, high], sums_dn.at[high], send_sem.at[9], sum_dn.at[g], (e, up)
        ).start()
        channels(dn)
        remote(
            partial.at[dn, low], sums_up.at[low], send_sem.at[10], sum_up.at[g], (e, dn)
        ).start()
        channels(y)

    def relay(g):
        low, high = pl.ds(g * BLOCKS, HALF), pl.ds(g * BLOCKS + HALF, HALF)
        slot = pl.ds(g * HALF, HALF)
        received(relay_dn.at[slot], rel_dn.at[g])
        partial[up, low] = (partial[up, low].astype(F32) + relay_dn[slot].astype(F32)).astype(BF16)
        remote(
            partial.at[up, low], sums_dn.at[low], send_sem.at[9], sum_dn.at[g], (e, up)
        ).start()
        received(relay_up.at[slot], rel_up.at[g])
        partial[dn, high] = (
            partial[dn, high].astype(F32) + relay_up[slot].astype(F32)
        ).astype(BF16)
        remote(
            partial.at[dn, high], sums_up.at[high], send_sem.at[10], sum_up.at[g], (e, dn)
        ).start()

    def give_back(g):
        span = pl.ds(g * BLOCKS, BLOCKS)
        received(sums_dn.at[span], sum_dn.at[g])
        received(sums_up.at[span], sum_up.at[g])
        final[span] = (
            partial[y, span].astype(F32) + sums_dn[span].astype(F32) + sums_up[span].astype(F32)
        ).astype(BF16)

        @pl.when(g == 3)
        def _():
            pltpu.make_async_copy(
                final.at[OWN_BLOCK], returned.at[OWN_BLOCK], ret_sem.at[3]
            ).start()

        def send(k, carry):
            remote(
                final.at[k], returned.at[k], send_sem.at[11], ret_sem.at[g], (behind(k), y)
            ).start()
            return carry

        lax.fori_loop(g * BLOCKS + jnp.where(g == 3, 1, 0), (g + 1) * BLOCKS, send, 0)

    def combine(g):
        span = pl.ds(g * BLOCKS, BLOCKS)
        received(returned.at[span], ret_sem.at[g])
        block = returned[span].reshape(ROWS, OWN)
        number = (lax.broadcasted_iota(jnp.int32, (256, 128), 1) + g * ROWS).astype(F32)

        def add(b, carry):
            at = pl.ds(pl.multiple_of(b * 256, 256), 256)
            place = place_col[at, :]
            chosen = jnp.concatenate(
                [(place == number).astype(F32), (place == number + 128.0).astype(F32)], axis=1
            ).astype(BF16)
            tile_rows = pl.ds(b * 8, 8)
            added = jnp.dot(chosen, block, preferred_element_type=F32)
            total[tile_rows] += added.reshape(8, SIDE, OWN)
            return carry

        lax.fori_loop(0, TOKENS // 256, add, 0)

    dispatch_far(0)
    remote(conv.at[y, pack], conv.at[y, pack], send_sem.at[16], src_sem.at[6], (e, up)).start()
    remote(conv.at[y, pack], conv.at[y, pack], send_sem.at[16], src_sem.at[7], (e, dn)).start()
    dispatch_far(1)
    dispatch_far(2)
    forward_pack()
    for load in loads[6:]:
        load.wait()

    def step(s, carry):
        pl.when((s < GROUPS) & jnp.logical_not(is_near(s)))(
            lambda: gather(s)
        )
        pl.when((s >= 1) & (s < GROUPS + 1) & jnp.logical_not(is_near(s - 1)))(
            lambda: forward(s - 1)
        )
        pl.when(s == 0)(conv_complete)
        pl.when((s >= 2) & (s < GROUPS + 2))(lambda: expert(s - 2))
        pl.when((s >= 3) & (s < GROUPS + 3))(lambda: relay(s - 3))
        pl.when((s >= 6) & (s < GROUPS + 6))(lambda: combine(s - 6))
        pl.when((s >= 4) & (s < GROUPS + 4))(lambda: give_back(s - 4))
        pl.when((s + 3 < GROUPS) & is_near(s + 3))(lambda: dispatch_near(s + 3))
        pl.when((s + 3 < GROUPS) & jnp.logical_not(is_near(s + 3)))(lambda: dispatch_far(s + 3))
        return carry

    lax.fori_loop(0, GROUPS + 6, step, 0)
    out[...] = total[...].reshape(TOKENS, OWN).astype(BF16)

    def span_of(count):
        return outgoing.at[0, pl.ds(0, count)]

    sent(rim_out.at[pl.ds(0, CHIPS - 1)], send_sem.at[0])
    sent(pick_out.at[pl.ds(0, CHIPS - 1)], send_sem.at[1])
    sent(rim_in.at[0], send_sem.at[13])
    sent(span_of(40), send_sem.at[2])
    sent(span_of(40), send_sem.at[3])
    sent(span_of(40), send_sem.at[4])
    sent(span_of(16), send_sem.at[5])
    sent(span_of(16), send_sem.at[6])
    sent(span_of(8), send_sem.at[18])
    sent(span_of(32), send_sem.at[7])
    sent(span_of(32), send_sem.at[8])
    sent(span_of(64), send_sem.at[9])
    sent(span_of(64), send_sem.at[10])
    sent(span_of(63), send_sem.at[11])
    sent(conv.at[pl.ds(0, 2), pl.ds(0, INNER)], send_sem.at[12])
    sent(conv.at[0, pl.ds(0, INNER)], send_sem.at[14])
    sent(outgoing.at[:, pl.ds(0, 23)], send_sem.at[15])
    sent(conv.at[0, pl.ds(0, 2 * EDGE)], send_sem.at[16])
    sent(conv.at[0, pl.ds(0, EDGE)], send_sem.at[17])


def shards(
    pixels,
    conv_weight,
    norm_gain,
    router_weight,
    gate_weight,
    up_weight,
    down_weight,
    expert_ids,
    neighbours,
):
    vmem = pl.BlockSpec(memory_space=pltpu.VMEM)
    hbm = pl.BlockSpec(memory_space=pltpu.HBM)
    blocks = (EXPERTS, CAP, OWN)
    per_group = pltpu.SemaphoreType.DMA((GROUPS,))
    return pl.pallas_call(
        kernel,
        out_shape=pltpu.VMEM((TOKENS, OWN), BF16),
        in_specs=[hbm] * 9,
        out_specs=vmem,
        scratch_shapes=[
            pltpu.VMEM((TOKENS, OWN), BF16),
            pltpu.VMEM((9, OWN), F32),
            pltpu.VMEM((1, WIDTH), F32),
            pltpu.VMEM((1, WIDTH), BF16),
            pltpu.VMEM((1, TOKENS), jnp.int32),
            pltpu.VMEM((1, 8), jnp.int32),
            pltpu.VMEM((SIDE + 2, SIDE + 2 * LEFT, OWN), F32),
            pltpu.VMEM((CHIPS, 16, 128), F32),
            pltpu.VMEM((CHIPS, 16, 128), BF16),
            pltpu.VMEM((2, CHIPS, 16, 128), BF16),
            pltpu.VMEM((2, CHIPS, 16, 128), F32),
            pltpu.VMEM((CHIPS, 16, 128), F32),
            pltpu.VMEM((CHIPS, 16, 128), BF16),
            pltpu.VMEM((CHIPS, 16, 128), BF16),
            pltpu.VMEM((PARTS, TOKENS + EDGE, OWN), BF16),
            pltpu.VMEM((8, TOKENS), F32),
            pltpu.VMEM((1, TOKENS + EDGE), F32),
            pltpu.VMEM((TOKENS, 128), F32),
            pltpu.VMEM((WIDTH, 128), BF16),
            pltpu.VMEM((WIDTH, UNITS), BF16),
            pltpu.VMEM((WIDTH, UNITS), BF16),
            pltpu.VMEM((UNITS, WIDTH), BF16),
            pltpu.VMEM((PARTS,) + blocks, BF16),
            pltpu.VMEM((PARTS,) + blocks, BF16),
            pltpu.VMEM((ROWS, WIDTH), BF16),
            pltpu.VMEM((ROWS, UNITS), BF16),
            pltpu.VMEM((PARTS,) + blocks, BF16),
            pltpu.VMEM((EXPERTS // 2, CAP, OWN), BF16),
            pltpu.VMEM((EXPERTS // 2, CAP, OWN), BF16),
            pltpu.VMEM(blocks, BF16),
            pltpu.VMEM(blocks, BF16),
            pltpu.VMEM(blocks, BF16),
            pltpu.VMEM(blocks, BF16),
            pltpu.VMEM((SIDE, SIDE, OWN), F32),
            pltpu.SemaphoreType.DMA((9,)),
            pltpu.SemaphoreType.DMA((19,)),
            pltpu.SemaphoreType.DMA((3,)),
            pltpu.SemaphoreType.DMA((10,)),
        ]
        + [per_group] * 10,
        compiler_params=pltpu.CompilerParams(
            collective_id=0, has_side_effects=True, vmem_limit_bytes=56 * 1024 * 1024
        ),
    )(
        pixels,
        conv_weight,
        norm_gain.reshape(1, WIDTH),
        router_weight.reshape(1, WIDTH),
        expert_ids.reshape(1, TOKENS),
        neighbours,
        gate_weight,
        up_weight,
        down_weight,
    )


def solution(mesh):
    in_specs = (
        P("expert", "hidden"),
        P(None, "hidden"),
        P(),
        P(None, "expert"),
        P("expert", None, "hidden"),
        P("expert", None, "hidden"),
        P("expert", "hidden", None),
        P("expert", None),
        P("expert", None),
    )
    out_specs = P("expert", "hidden")
    return jax.shard_map(shards, mesh=mesh, in_specs=in_specs, out_specs=out_specs, check_vma=False)
```

```python
import jax
import jax.numpy as jnp
from jax import lax
from jax.experimental import pallas as pl
from jax.experimental.pallas import tpu as pltpu
from jax.sharding import PartitionSpec as P

MESH = pl.DeviceIdType.MESH
F32 = jnp.float32
BF16 = jnp.bfloat16

SIDE = 32
TOKENS = SIDE * SIDE
EXPERTS = 64
CAP = 32
OWN = 256
PARTS = 4
UNITS = 1024
WIDTH = OWN * PARTS
GROUPS = 8
BLOCKS = EXPERTS // GROUPS
HALF = BLOCKS // 2
ROWS = BLOCKS * CAP
CHIPS = EXPERTS // 2
EDGE = 4 * SIDE
INNER = TOKENS - 2 * SIDE
OWN_BLOCK = 24
LEFT = 8
EPSILON = 1e-05


def kernel(
    pixels,
    conv_weight,
    norm_gain,
    router,
    ids,
    table,
    gate_hbm,
    up_hbm,
    down_hbm,
    out,
    pixels_in,
    taps,
    gain_in,
    router_in,
    ids_in,
    table_in,
    padded,
    rim_wide,
    rim_out,
    rim_in,
    held,
    pick_wide,
    pick_out,
    pick_in,
    conv,
    parts_row,
    place_row,
    place_col,
    router_wide,
    gate_w,
    up_w,
    down_w,
    outgoing,
    rows,
    normed,
    hidden,
    partial,
    relay_dn,
    relay_up,
    sums_dn,
    sums_up,
    final,
    returned,
    total,
    load_sem,
    send_sem,
    rim_sem,
    src_sem,
    disp_sem,
    gat_dn,
    gat_up,
    fwd_dn,
    fwd_up,
    rel_dn,
    rel_up,
    sum_dn,
    sum_up,
    ret_sem,
):
    e = lax.axis_index("expert")
    y = lax.axis_index("hidden")
    x, z, c = lax.div(e, 16), lax.rem(lax.div(e, 2), 8), lax.rem(e, 2)
    chip = lax.div(e, 2)
    up, dn, op = lax.rem(y + 1, 4), lax.rem(y + 3, 4), lax.rem(y + 2, 4)

    def is_near(g):
        return (g == 3) | (g == 5) | (g == 7)

    def offsets(k):
        g, i = lax.div(k, BLOCKS), lax.rem(k, BLOCKS)
        dc = lax.rem(i, 2)
        third = lax.rem(i + lax.div(g + 5, 2) + 2, 3)
        hops = jnp.where((g == 0) | (g == 6), 2, jnp.where(g == 4, 4, 3))
        flip = lax.rem(dc + jnp.where((g == 2) | (g == 6), 1, 0), 2)
        far_dz = jnp.where(flip == 1, 8 - hops, hops)
        dz = jnp.where(is_near(g), jnp.where(third == 2, 7, third), far_dz)
        return lax.div(i, 2), dc, dz

    def ahead(k):
        dx, dc, dz = offsets(k)
        return (lax.rem(x + dx, 4) * 8 + lax.rem(z + dz, 8)) * 2 + lax.rem(c + dc, 2)

    def behind(k):
        dx, dc, dz = offsets(k)
        return (lax.rem(x + 4 - dx, 4) * 8 + lax.rem(z + 8 - dz, 8)) * 2 + lax.rem(c + dc, 2)

    def chip_ahead(k):
        return lax.rem(x + lax.div(k, 8), 4) * 8 + lax.rem(z + lax.rem(k, 8), 8)

    def remote(src, dst, sent, got, target):
        return pltpu.make_async_remote_copy(
            src_ref=src,
            dst_ref=dst,
            send_sem=sent,
            recv_sem=got,
            device_id=target,
            device_id_type=MESH,
        )

    def received(dst, sem):
        remote(dst, dst, send_sem.at[0], sem, (e, up)).wait_recv()

    def sent(src, sem):
        remote(src, src, sem, rim_sem.at[0], (e, up)).wait_send()

    loads = [
        pltpu.make_async_copy(source, target, load_sem.at[i])
        for i, (source, target) in enumerate(
            (
                (pixels, pixels_in),
                (table, table_in),
                (ids, ids_in),
                (router, router_in),
                (conv_weight, taps),
                (norm_gain, gain_in),
                (gate_hbm.at[0], gate_w),
                (up_hbm.at[0], up_w),
                (down_hbm.at[0], down_w),
            )
        )
    ]
    for load in loads:
        load.start()

    barrier = pltpu.get_barrier_semaphore()

    def greet(k, carry):
        target = lax.rem(e + k, EXPERTS)
        pl.semaphore_signal(barrier, inc=1, device_id=(target, y), device_id_type=MESH)
        return carry

    lax.fori_loop(1, EXPERTS, greet, 0)
    pl.semaphore_signal(barrier, inc=1, device_id=(e, up), device_id_type=MESH)
    pl.semaphore_signal(barrier, inc=1, device_id=(e, dn), device_id_type=MESH)

    padded[...] = jnp.zeros_like(padded)
    rim_wide[...] = jnp.zeros_like(rim_wide)
    conv[:, 0:SIDE] = jnp.zeros((PARTS, SIDE, OWN), BF16)
    conv[:, TOKENS - SIDE : TOKENS] = jnp.zeros((PARTS, SIDE, OWN), BF16)
    for load in loads[:6]:
        load.wait()

    def widen(i, carry):
        at = pl.multiple_of(i * SIDE, SIDE)
        padded[i + 1, LEFT : LEFT + SIDE, :] = pixels_in[pl.ds(at, SIDE), :].astype(F32)
        return carry

    lax.fori_loop(0, SIDE, widen, 0)
    near, far = LEFT, LEFT + SIDE - 1
    for half in range(2):
        lanes = slice(128 * half, 128 * half + 128)
        rim_wide[:, half, :] = padded[1, near : far + 1, lanes]
        rim_wide[:, 2 + half, :] = padded[SIDE, near : far + 1, lanes]
        rim_wide[:, 4 + half, :] = padded[1 : SIDE + 1, near, lanes]
        rim_wide[:, 6 + half, :] = padded[1 : SIDE + 1, far, lanes]
    rim_wide[:, 8, 0:8] = jnp.broadcast_to(table_in[...].astype(F32), (CHIPS, 8))
    rim_out[...] = rim_wide[...].astype(BF16)
    rim_in[c, chip] = rim_out[chip]

    def convolve(i, carry):
        mixed = padded[i + 1, near : far + 1, :]
        for a in range(3):
            for b in range(3):
                tap = taps[3 * a + b : 3 * a + b + 1, :]
                mixed = mixed + tap * padded[i + a, near - 1 + b : far + b, :]
        rounded = mixed.astype(BF16)
        conv[y, pl.ds(pl.multiple_of(i * SIDE, SIDE), SIDE), :] = rounded
        total[i] = rounded.astype(F32)
        return carry

    lax.fori_loop(0, SIDE, convolve, 0)

    pl.semaphore_wait(barrier, EXPERTS - 1 + 2)

    def send_rim(k, carry):
        target = chip_ahead(k)
        remote(
            rim_out.at[target],
            rim_in.at[c, chip],
            send_sem.at[0],
            rim_sem.at[0],
            (target * 2 + c, y),
        ).start()
        return carry

    lax.fori_loop(1, CHIPS, send_rim, 0)

    first_half, second_half = pl.ds(SIDE, INNER // 2), pl.ds(SIDE + INNER // 2, INNER // 2)
    remote(
        conv.at[y, first_half], conv.at[y, first_half], send_sem.at[12], src_sem.at[0], (e, up)
    ).start()
    remote(
        conv.at[y, second_half], conv.at[y, second_half], send_sem.at[12], src_sem.at[1], (e, dn)
    ).start()
    remote(
        conv.at[y, second_half], conv.at[y, second_half], send_sem.at[12], src_sem.at[2], (e, up)
    ).start()
    remote(
        conv.at[y, first_half], conv.at[y, first_half], send_sem.at[12], src_sem.at[3], (e, dn)
    ).start()

    onehot = (
        ids_in[...] == lax.broadcasted_iota(jnp.int32, (EXPERTS, TOKENS), 0)
    ).astype(F32)
    onehot_bf = onehot.astype(BF16)
    parts_row[...] = jnp.zeros_like(parts_row)

    def places(b, carry):
        at = pl.multiple_of(b * 256, 256)
        earlier = lax.broadcasted_iota(jnp.int32, (TOKENS, 256), 0) < (
            lax.broadcasted_iota(jnp.int32, (TOKENS, 256), 1) + at
        )
        counts = jnp.dot(
            onehot_bf, earlier.astype(F32).astype(BF16), preferred_element_type=F32
        )
        own = ids_in[0:1, pl.ds(at, 256)]
        chosen = own == lax.broadcasted_iota(jnp.int32, (EXPERTS, 256), 0)
        slot = jnp.sum(jnp.where(chosen, counts, 0.0), axis=0, keepdims=True)
        dx = (lax.shift_right_logical(own, 4) - x + 4) & 3
        dz = ((lax.shift_right_logical(own, 1) & 7) - z + 8) & 7
        dc = ((own & 1) + c) & 1
        i = dx * 2 + dc
        third = jnp.where(dz == 7, 2, dz) + 9 - i
        third = jnp.where(third >= 6, third - 6, third)
        third = jnp.where(third >= 3, third - 3, third)
        is_close = (dz <= 1) | (dz == 7)
        flip = jnp.where(dz > 4, 1, 0) ^ dc
        far_group = jnp.where(
            dz == 4, 4, jnp.where((dz == 2) | (dz == 6), 6 * flip, 1 + flip)
        )
        group = jnp.where(is_close, 3 + 2 * third, far_group)
        block = (group * BLOCKS + i).astype(F32)
        place = block * CAP + slot
        number = lax.broadcasted_iota(jnp.int32, (1, 256), 1) + at
        row, column = lax.shift_right_logical(number, 5), number & 31
        inner = (row >= 1) & (row <= SIDE - 2) & (column >= 1) & (column <= SIDE - 2)
        place_row[0:1, pl.ds(at, 256)] = jnp.where(inner, place, -1.0)
        parts_row[0:1, pl.ds(at, 256)] = block
        parts_row[1:2, pl.ds(at, 256)] = slot
        place_col[pl.ds(at, 256), :] = jnp.broadcast_to(place, (128, 256)).T
        return carry

    lax.fori_loop(0, TOKENS // 256, places, 0)

    number = lax.broadcasted_iota(jnp.int32, (1, EDGE), 1)
    along = number & 31
    edge = lax.shift_right_logical(number, 5)
    pixel = jnp.where(
        edge == 0,
        along,
        jnp.where(
            edge == 1,
            along + (TOKENS - SIDE),
            jnp.where(edge == 2, along * SIDE, along * SIDE + SIDE - 1),
        ),
    )
    picks = (lax.broadcasted_iota(jnp.int32, (TOKENS, EDGE), 0) == pixel).astype(F32).astype(BF16)
    border = jnp.dot(parts_row[...].astype(BF16), picks, preferred_element_type=F32)
    counted = (edge <= 1) | ((along >= 1) & (along <= SIDE - 2))
    place_row[0:1, TOKENS : TOKENS + EDGE] = jnp.where(
        counted, border[0:1] * CAP + border[1:2], -1.0
    )

    def widen_router(b, carry):
        at = pl.multiple_of(b * 256, 256)
        column = router_in[0:1, pl.ds(at, 256)].astype(F32)
        router_wide[pl.ds(at, 256), :] = jnp.broadcast_to(column, (128, 256)).T.astype(BF16)
        return carry

    received(rim_in.at[c, pl.ds(0, CHIPS - 1)], rim_sem.at[0])
    other = e + 1 - 2 * c
    remote(rim_in.at[c], rim_in.at[c], send_sem.at[13], rim_sem.at[2], (other, y)).start()
    held[c] = rim_in[c].astype(F32)
    received(rim_in.at[1 - c], rim_sem.at[2])
    held[1 - c] = rim_in[1 - c].astype(F32)
    tables = held[c, :, 8, :]
    tile = lax.broadcasted_iota(jnp.int32, (CHIPS, EXPERTS), 1)
    tile = ((tile & 31) * 2 + lax.shift_right_logical(tile, 5)).astype(F32)
    edges = [
        jnp.concatenate(
            [
                jnp.concatenate([held[core, :, 2 * side + half, :] for half in range(2)], axis=1)
                for core in range(2)
            ],
            axis=0,
        ).astype(BF16)
        for side in range(4)
    ]
    for direction, side in enumerate((1, 0, 3, 2, 1, 1, 0, 0)):
        chosen = (tables[:, direction : direction + 1] == tile).astype(F32).astype(BF16)
        found = jnp.dot(chosen, edges[side], preferred_element_type=F32)
        pick_wide[:, 2 * direction, :] = found[:, 0:128]
        pick_wide[:, 2 * direction + 1, :] = found[:, 128:256]
    pick_out[...] = pick_wide[...].astype(BF16)

    def send_pick(k, carry):
        target = chip_ahead(k)
        remote(
            pick_out.at[target],
            pick_in.at[chip],
            send_sem.at[1],
            rim_sem.at[1],
            (target * 2 + c, y),
        ).start()
        return carry

    lax.fori_loop(1, CHIPS, send_pick, 0)
    pick_in[chip] = pick_out[chip]

    lax.fori_loop(0, WIDTH // 256, widen_router, 0)
    received(conv.at[dn, first_half], src_sem.at[0])
    remote(
        conv.at[dn, first_half], conv.at[dn, first_half], send_sem.at[14], src_sem.at[4], (e, up)
    ).start()
    received(conv.at[up, second_half], src_sem.at[1])
    remote(
        conv.at[up, second_half], conv.at[up, second_half], send_sem.at[14], src_sem.at[5], (e, dn)
    ).start()

    received(pick_in.at[pl.ds(0, CHIPS - 1)], rim_sem.at[1])
    pick_wide[...] = pick_in[...].astype(F32)
    for half in range(2):
        lanes = slice(128 * half, 128 * half + 128)
        padded[0, near : far + 1, lanes] = pick_wide[:, half, :]
        padded[SIDE + 1, near : far + 1, lanes] = pick_wide[:, 2 + half, :]
        padded[1 : SIDE + 1, near - 1, lanes] = pick_wide[:, 4 + half, :]
        padded[1 : SIDE + 1, far + 1, lanes] = pick_wide[:, 6 + half, :]
        last = SIDE - 1
        padded[0, near - 1 : near, lanes] = pick_wide[last, 8 + half : 9 + half, :]
        padded[0, far + 1 : far + 2, lanes] = pick_wide[0, 10 + half : 11 + half, :]
        padded[SIDE + 1, near - 1 : near, lanes] = pick_wide[last, 12 + half : 13 + half, :]
        padded[SIDE + 1, far + 1 : far + 2, lanes] = pick_wide[0, 14 + half : 15 + half, :]

    def mix(center, window):
        mixed = center
        for a in range(3):
            for b in range(3):
                mixed = mixed + taps[3 * a + b : 3 * a + b + 1, :] * window(a, b)
        return mixed.astype(BF16)

    left = mix(
        padded[1 : SIDE + 1, near, :], lambda a, b: padded[a : a + SIDE, near - 1 + b, :]
    )
    right = mix(padded[1 : SIDE + 1, far, :], lambda a, b: padded[a : a + SIDE, far - 1 + b, :])
    top = mix(padded[1, near : far + 1, :], lambda a, b: padded[a, near - 1 + b : far + b, :])
    bottom = mix(
        padded[SIDE, near : far + 1, :],
        lambda a, b: padded[SIDE - 1 + a, near - 1 + b : far + b, :],
    )
    for i, strip in enumerate((top, bottom, left, right)):
        conv[y, TOKENS + i * SIDE : TOKENS + (i + 1) * SIDE, :] = strip
    total[:, 0, :] = left.astype(F32)
    total[:, SIDE - 1, :] = right.astype(F32)
    total[0] = top.astype(F32)
    total[SIDE - 1] = bottom.astype(F32)

    def blocks_of(g):
        first = lax.broadcasted_iota(jnp.int32, (ROWS, TOKENS + EDGE), 0) + g * ROWS
        return (place_row[...] == first.astype(F32)).astype(F32).astype(BF16)

    def dispatch_far(g):
        block = jnp.dot(blocks_of(g), conv[y], preferred_element_type=F32).astype(BF16)
        outgoing[y, pl.ds(g * BLOCKS, BLOCKS)] = block.reshape(BLOCKS, CAP, OWN)

        def send(k, carry):
            remote(
                outgoing.at[y, k], rows.at[y, k], send_sem.at[2], disp_sem.at[g], (ahead(k), y)
            ).start()
            return carry

        lax.fori_loop(g * BLOCKS, (g + 1) * BLOCKS, send, 0)

    def dispatch_near(g):
        chosen = blocks_of(g)
        for part in range(PARTS):
            block = jnp.dot(chosen, conv[part], preferred_element_type=F32).astype(BF16)
            outgoing[part, pl.ds(g * BLOCKS, BLOCKS)] = block.reshape(BLOCKS, CAP, OWN)

        @pl.when(g == 3)
        def _():
            pltpu.make_async_copy(
                outgoing.at[:, OWN_BLOCK], rows.at[:, OWN_BLOCK], disp_sem.at[3]
            ).start()

        def send(k, carry):
            remote(
                outgoing.at[:, k], rows.at[:, k], send_sem.at[15], disp_sem.at[g], (ahead(k), y)
            ).start()
            return carry

        lax.fori_loop(g * BLOCKS + jnp.where(g == 3, 1, 0), (g + 1) * BLOCKS, send, 0)

    pack = pl.ds(TOKENS, EDGE)
    pack_low, pack_high = pl.ds(TOKENS, EDGE // 2), pl.ds(TOKENS + EDGE // 2, EDGE // 2)

    def forward_pack():
        received(conv.at[dn, pack], src_sem.at[6])
        remote(
            conv.at[dn, pack_low], conv.at[dn, pack_low], send_sem.at[17], src_sem.at[8], (e, up)
        ).start()
        received(conv.at[up, pack], src_sem.at[7])
        remote(
            conv.at[up, pack_high], conv.at[up, pack_high], send_sem.at[17], src_sem.at[9], (e, dn)
        ).start()

    def conv_complete():
        received(conv.at[dn, second_half], src_sem.at[2])
        received(conv.at[up, first_half], src_sem.at[3])
        received(conv.at[op, first_half], src_sem.at[4])
        received(conv.at[op, second_half], src_sem.at[5])
        received(conv.at[op, pack_low], src_sem.at[8])
        received(conv.at[op, pack_high], src_sem.at[9])

    def gather(g):
        span = pl.ds(g * BLOCKS, BLOCKS)
        mine = rows.at[y, span]
        received(mine, disp_sem.at[g])
        remote(mine, mine, send_sem.at[3], gat_dn.at[g], (e, up)).start()
        remote(mine, mine, send_sem.at[4], gat_up.at[g], (e, dn)).start()

        @pl.when(g == 0)
        def _():
            remote(mine, mine, send_sem.at[18], fwd_dn.at[0], (e, op)).start()

    def forward(g):
        received(rows.at[dn, pl.ds(g * BLOCKS, BLOCKS)], gat_dn.at[g])

        @pl.when(g > 0)
        def _():
            low = rows.at[dn, pl.ds(g * BLOCKS, HALF)]
            remote(low, low, send_sem.at[5], fwd_dn.at[g], (e, up)).start()

        received(rows.at[up, pl.ds(g * BLOCKS, BLOCKS)], gat_up.at[g])

        @pl.when(g > 0)
        def _():
            high = rows.at[up, pl.ds(g * BLOCKS + HALF, HALF)]
            remote(high, high, send_sem.at[6], fwd_up.at[g], (e, dn)).start()

    def arrived(g):
        @pl.when(g == 0)
        def _():
            received(rows.at[op, pl.ds(g * BLOCKS, BLOCKS)], fwd_dn.at[g])

        @pl.when(g > 0)
        def _():
            received(rows.at[op, pl.ds(g * BLOCKS, HALF)], fwd_dn.at[g])
            received(rows.at[op, pl.ds(g * BLOCKS + HALF, HALF)], fwd_up.at[g])

    def expert(g):
        span = pl.ds(g * BLOCKS, BLOCKS)
        pl.when(is_near(g))(lambda: received(rows.at[:, span], disp_sem.at[g]))
        pl.when(jnp.logical_not(is_near(g)))(lambda: arrived(g))
        squares = jnp.zeros((ROWS, 1), F32)
        for part in range(PARTS):
            wide = rows[part, span].reshape(ROWS, OWN).astype(F32)
            squares = squares + jnp.sum(wide * wide, axis=1, keepdims=True)
        scale = lax.rsqrt(squares * (1.0 / WIDTH) + EPSILON)
        for part in range(PARTS):
            wide = rows[part, span].reshape(ROWS, OWN).astype(F32)
            normed[:, part * OWN : (part + 1) * OWN] = (
                wide * scale * gain_in[0:1, part * OWN : (part + 1) * OWN]
            ).astype(BF16)
        score = jnp.dot(normed[...], router_wide[...], preferred_element_type=F32)
        weight = 1.0 / (1.0 + jnp.exp(-score))
        weight = jnp.concatenate([weight, weight], axis=1)

        def units(n, carry):
            at = pl.ds(pl.multiple_of(n * 256, 256), 256)
            gate = jnp.dot(normed[...], gate_w[:, at], preferred_element_type=F32)
            lift = jnp.dot(normed[...], up_w[:, at], preferred_element_type=F32)
            hidden[:, at] = (gate / (1.0 + jnp.exp(-gate)) * lift * weight).astype(BF16)
            return carry

        lax.fori_loop(0, UNITS // 256, units, 0)

        def channels(part):
            at = pl.ds(pl.multiple_of(part * OWN, OWN), OWN)
            result = jnp.dot(hidden[...], down_w[:, at], preferred_element_type=F32)
            partial[part, span] = result.astype(BF16).reshape(BLOCKS, CAP, OWN)

        low, high = pl.ds(g * BLOCKS, HALF), pl.ds(g * BLOCKS + HALF, HALF)
        slot = pl.ds(g * HALF, HALF)
        channels(op)
        remote(
            partial.at[op, low], relay_dn.at[slot], send_sem.at[7], rel_dn.at[g], (e, up)
        ).start()
        remote(
            partial.at[op, high], relay_up.at[slot], send_sem.at[8], rel_up.at[g], (e, dn)
        ).start()
        channels(up)
        remote(
            partial.at[up, high], sums_dn.at[high], send_sem.at[9], sum_dn.at[g], (e, up)
        ).start()
        channels(dn)
        remote(
            partial.at[dn, low], sums_up.at[low], send_sem.at[10], sum_up.at[g], (e, dn)
        ).start()
        channels(y)

    def relay(g):
        low, high = pl.ds(g * BLOCKS, HALF), pl.ds(g * BLOCKS + HALF, HALF)
        slot = pl.ds(g * HALF, HALF)
        received(relay_dn.at[slot], rel_dn.at[g])
        partial[up, low] = (partial[up, low].astype(F32) + relay_dn[slot].astype(F32)).astype(BF16)
        remote(
            partial.at[up, low], sums_dn.at[low], send_sem.at[9], sum_dn.at[g], (e, up)
        ).start()
        received(relay_up.at[slot], rel_up.at[g])
        partial[dn, high] = (
            partial[dn, high].astype(F32) + relay_up[slot].astype(F32)
        ).astype(BF16)
        remote(
            partial.at[dn, high], sums_up.at[high], send_sem.at[10], sum_up.at[g], (e, dn)
        ).start()

    def give_back(g):
        span = pl.ds(g * BLOCKS, BLOCKS)
        received(sums_dn.at[span], sum_dn.at[g])
        received(sums_up.at[span], sum_up.at[g])
        final[span] = (
            partial[y, span].astype(F32) + sums_dn[span].astype(F32) + sums_up[span].astype(F32)
        ).astype(BF16)

        @pl.when(g == 3)
        def _():
            pltpu.make_async_copy(
                final.at[OWN_BLOCK], returned.at[OWN_BLOCK], ret_sem.at[3]
            ).start()

        def send(k, carry):
            remote(
                final.at[k], returned.at[k], send_sem.at[11], ret_sem.at[g], (behind(k), y)
            ).start()
            return carry

        lax.fori_loop(g * BLOCKS + jnp.where(g == 3, 1, 0), (g + 1) * BLOCKS, send, 0)

    def combine(g):
        span = pl.ds(g * BLOCKS, BLOCKS)
        received(returned.at[span], ret_sem.at[g])
        block = returned[span].reshape(ROWS, OWN)
        number = (lax.broadcasted_iota(jnp.int32, (256, 128), 1) + g * ROWS).astype(F32)

        def add(b, carry):
            at = pl.ds(pl.multiple_of(b * 256, 256), 256)
            place = place_col[at, :]
            chosen = jnp.concatenate(
                [(place == number).astype(F32), (place == number + 128.0).astype(F32)], axis=1
            ).astype(BF16)
            tile_rows = pl.ds(b * 8, 8)
            added = jnp.dot(chosen, block, preferred_element_type=F32)
            total[tile_rows] += added.reshape(8, SIDE, OWN)
            return carry

        lax.fori_loop(0, TOKENS // 256, add, 0)

    dispatch_far(0)
    remote(conv.at[y, pack], conv.at[y, pack], send_sem.at[16], src_sem.at[6], (e, up)).start()
    remote(conv.at[y, pack], conv.at[y, pack], send_sem.at[16], src_sem.at[7], (e, dn)).start()
    dispatch_far(1)
    dispatch_far(2)
    forward_pack()
    for load in loads[6:]:
        load.wait()

    def step(s, carry):
        pl.when((s < GROUPS) & jnp.logical_not(is_near(s)))(
            lambda: gather(s)
        )
        pl.when((s >= 1) & (s < GROUPS + 1) & jnp.logical_not(is_near(s - 1)))(
            lambda: forward(s - 1)
        )
        pl.when(s == 0)(conv_complete)
        pl.when((s >= 2) & (s < GROUPS + 2))(lambda: expert(s - 2))
        pl.when((s >= 3) & (s < GROUPS + 3))(lambda: relay(s - 3))
        pl.when((s >= GROUPS + 2) & (s < GROUPS + 4))(lambda: give_back(s - 4))
        pl.when((s >= 6) & (s < GROUPS + 6))(lambda: combine(s - 6))
        pl.when((s >= 4) & (s < GROUPS + 2))(lambda: give_back(s - 4))
        pl.when((s + 3 < GROUPS) & is_near(s + 3))(lambda: dispatch_near(s + 3))
        pl.when((s + 3 < GROUPS) & jnp.logical_not(is_near(s + 3)))(lambda: dispatch_far(s + 3))
        return carry

    lax.fori_loop(0, GROUPS + 6, step, 0)
    out[...] = total[...].reshape(TOKENS, OWN).astype(BF16)

    def span_of(count):
        return outgoing.at[0, pl.ds(0, count)]

    sent(rim_out.at[pl.ds(0, CHIPS - 1)], send_sem.at[0])
    sent(pick_out.at[pl.ds(0, CHIPS - 1)], send_sem.at[1])
    sent(rim_in.at[0], send_sem.at[13])
    sent(span_of(40), send_sem.at[2])
    sent(span_of(40), send_sem.at[3])
    sent(span_of(40), send_sem.at[4])
    sent(span_of(16), send_sem.at[5])
    sent(span_of(16), send_sem.at[6])
    sent(span_of(8), send_sem.at[18])
    sent(span_of(32), send_sem.at[7])
    sent(span_of(32), send_sem.at[8])
    sent(span_of(64), send_sem.at[9])
    sent(span_of(64), send_sem.at[10])
    sent(span_of(63), send_sem.at[11])
    sent(conv.at[pl.ds(0, 2), pl.ds(0, INNER)], send_sem.at[12])
    sent(conv.at[0, pl.ds(0, INNER)], send_sem.at[14])
    sent(outgoing.at[:, pl.ds(0, 23)], send_sem.at[15])
    sent(conv.at[0, pl.ds(0, 2 * EDGE)], send_sem.at[16])
    sent(conv.at[0, pl.ds(0, EDGE)], send_sem.at[17])


def shards(
    pixels,
    conv_weight,
    norm_gain,
    router_weight,
    gate_weight,
    up_weight,
    down_weight,
    expert_ids,
    neighbours,
):
    vmem = pl.BlockSpec(memory_space=pltpu.VMEM)
    hbm = pl.BlockSpec(memory_space=pltpu.HBM)
    blocks = (EXPERTS, CAP, OWN)
    per_group = pltpu.SemaphoreType.DMA((GROUPS,))
    return pl.pallas_call(
        kernel,
        out_shape=pltpu.VMEM((TOKENS, OWN), BF16),
        in_specs=[hbm] * 9,
        out_specs=vmem,
        scratch_shapes=[
            pltpu.VMEM((TOKENS, OWN), BF16),
            pltpu.VMEM((9, OWN), F32),
            pltpu.VMEM((1, WIDTH), F32),
            pltpu.VMEM((1, WIDTH), BF16),
            pltpu.VMEM((1, TOKENS), jnp.int32),
            pltpu.VMEM((1, 8), jnp.int32),
            pltpu.VMEM((SIDE + 2, SIDE + 2 * LEFT, OWN), F32),
            pltpu.VMEM((CHIPS, 16, 128), F32),
            pltpu.VMEM((CHIPS, 16, 128), BF16),
            pltpu.VMEM((2, CHIPS, 16, 128), BF16),
            pltpu.VMEM((2, CHIPS, 16, 128), F32),
            pltpu.VMEM((CHIPS, 16, 128), F32),
            pltpu.VMEM((CHIPS, 16, 128), BF16),
            pltpu.VMEM((CHIPS, 16, 128), BF16),
            pltpu.VMEM((PARTS, TOKENS + EDGE, OWN), BF16),
            pltpu.VMEM((8, TOKENS), F32),
            pltpu.VMEM((1, TOKENS + EDGE), F32),
            pltpu.VMEM((TOKENS, 128), F32),
            pltpu.VMEM((WIDTH, 128), BF16),
            pltpu.VMEM((WIDTH, UNITS), BF16),
            pltpu.VMEM((WIDTH, UNITS), BF16),
            pltpu.VMEM((UNITS, WIDTH), BF16),
            pltpu.VMEM((PARTS,) + blocks, BF16),
            pltpu.VMEM((PARTS,) + blocks, BF16),
            pltpu.VMEM((ROWS, WIDTH), BF16),
            pltpu.VMEM((ROWS, UNITS), BF16),
            pltpu.VMEM((PARTS,) + blocks, BF16),
            pltpu.VMEM((EXPERTS // 2, CAP, OWN), BF16),
            pltpu.VMEM((EXPERTS // 2, CAP, OWN), BF16),
            pltpu.VMEM(blocks, BF16),
            pltpu.VMEM(blocks, BF16),
            pltpu.VMEM(blocks, BF16),
            pltpu.VMEM(blocks, BF16),
            pltpu.VMEM((SIDE, SIDE, OWN), F32),
            pltpu.SemaphoreType.DMA((9,)),
            pltpu.SemaphoreType.DMA((19,)),
            pltpu.SemaphoreType.DMA((3,)),
            pltpu.SemaphoreType.DMA((10,)),
        ]
        + [per_group] * 10,
        compiler_params=pltpu.CompilerParams(
            collective_id=0, has_side_effects=True, vmem_limit_bytes=56 * 1024 * 1024
        ),
    )(
        pixels,
        conv_weight,
        norm_gain.reshape(1, WIDTH),
        router_weight.reshape(1, WIDTH),
        expert_ids.reshape(1, TOKENS),
        neighbours,
        gate_weight,
        up_weight,
        down_weight,
    )


def solution(mesh):
    in_specs = (
        P("expert", "hidden"),
        P(None, "hidden"),
        P(),
        P(None, "expert"),
        P("expert", None, "hidden"),
        P("expert", None, "hidden"),
        P("expert", "hidden", None),
        P("expert", None),
        P("expert", None),
    )
    out_specs = P("expert", "hidden")
    return jax.shard_map(shards, mesh=mesh, in_specs=in_specs, out_specs=out_specs, check_vma=False)
```
